32 devices in a mesh: row: 8 (over z, x), col: 4 (over y, core).
Axes of the slice: x: 2, y: 2, z: 4, core: 2. Of those that a mesh axis runs over, the one named last changes fastest.
Arguments:
- factor: float32 [8192, 8192], P('row', 'col'), may hold values from -0.24 to 0.24
- adjoint: float32 [8192, 8192], P('row', 'col'), may hold values from -6 to 6
- inverse: float32 [2, 256, 256], replicated, may hold values from -1 to 3, as said below
Outputs:
- adjoint_out: float32 [8192, 8192], P('row', 'col')
The draws below stay inside these ranges and needn't reach their ends.
Inputs may be any that keep to these rules, and one draw needn't show every extreme that they name: Each inverse[j] is lower triangular, with every diagonal entry larger than the sum of the magnitudes of the other entries of its row.
All inputs are finite; a program needn't handle non-finite values.
Results may differ from the reference program's by a relative error of at most 0.00011.
Values sent between devices are 32-bit elements; how exact they have to be, the bound alone decides.
A program may use at most 128 MiB of HBM per device.

```python
import jax
import jax.numpy as jnp
from jax import lax

NB = 256
TPR = 4
TPC = 8
NT = 32
N = 8192
N_ROW = 8
N_COL = 4


def draw_inverse(key, part):
    key_off, key_diag = jax.random.split(key)
    off_part = jax.random.uniform(key_off, (2, NB, NB), jnp.float32, -1.0, 1.0) * (1.2 / NB)
    diag_part = jax.random.uniform(key_diag, (2, NB), jnp.float32, 1.0, 2.0)
    strict_lower = jnp.tril(off_part, -1)
    return strict_lower + diag_part[:, :, None] * jnp.eye(NB, dtype=jnp.float32)


def shard_levels(stream_key, extent, shards, smallest, top_value):
    gain, own = 1.0, jax.random.fold_in(stream_key, 6)
    for dim, parts in shards:
        draws = jnp.exp(jax.random.uniform(jax.random.fold_in(own, dim), (parts,), jnp.float32, smallest / len(shards), top_value / len(shards)))
        gain = gain * jnp.repeat(draws, extent[dim] // parts).reshape([-1 if axis == dim else 1 for axis in range(len(extent))])
    return gain


def normal_values(rng, shape, width, reach, cuts=(), kind=jnp.bfloat16):
    values = jax.random.normal(rng, shape, jnp.float32) * width
    if len(cuts) > 0:
        values = shard_levels(rng, shape, cuts, -0.22, 0.18) * values
    return jnp.clip(values, min=-reach, max=reach).astype(kind)


def setup_inputs(seed: int = 0) -> dict:
    streams_of = jax.random.split(jax.random.key(seed), 4)
    factor = normal_values(streams_of[0], (N, N), 0.04, 0.24, ((0, 8), (1, 4)), jnp.float32)
    adjoint = normal_values(streams_of[1], (N, N), 1.0, 6.0, ((0, 8), (1, 4)), jnp.float32)
    inverse = draw_inverse(jax.random.fold_in(streams_of[3], 71), 0)
    return dict(factor=factor, adjoint=adjoint, inverse=inverse)


def matmul_high(left, right):
    return jnp.dot(left.astype(jnp.float32), right.astype(jnp.float32), precision=lax.Precision.HIGHEST, preferred_element_type=jnp.float32)

def halved_lower(matrix):
    return jnp.tril(matrix) - 0.5 * jnp.diag(jnp.diagonal(matrix))

def to_global(stored):
    blocks = stored.reshape(N_ROW, TPR, NB, N_COL, TPC, NB).transpose(1, 0, 2, 4, 3, 5)
    return blocks.reshape(NT * NB, NT * NB)

def to_stored(matrix):
    blocks = matrix.reshape(TPR, N_ROW, NB, TPC, N_COL, NB).transpose(1, 0, 2, 4, 3, 5)
    return blocks.reshape(NT * NB, NT * NB)

def reference(factor, adjoint, inverse):
    full_factor = to_global(factor)
    grad = to_global(adjoint)
    identity = jnp.eye(NB, dtype=jnp.float32)
    for position, panel_tile in enumerate((NT // 2, NT // 2 - 1)):
        start = panel_tile * NB
        finish = start + NB
        inverse_tile = inverse[position]
        factor_diag = lax.linalg.triangular_solve(inverse_tile, identity, left_side=True, lower=True)
        offdiag = matmul_high(grad[finish:, start:finish], inverse_tile)
        factor_row = full_factor[start:finish, :start]
        new_trailing = grad[finish:, :start] - matmul_high(offdiag, factor_row)
        dprime = jnp.tril(grad[start:finish, start:finish] - matmul_high(offdiag.T, full_factor[finish:, start:finish]))
        wmat = matmul_high(matmul_high(inverse_tile.T, halved_lower(matmul_high(factor_diag.T, dprime))), inverse_tile)
        sym = wmat + wmat.T
        new_row = grad[start:finish, :start] - matmul_high(offdiag.T, full_factor[finish:, :start]) - matmul_high(sym, factor_row)
        grad = grad.at[finish:, :start].set(new_trailing)
        grad = grad.at[start:finish, :start].set(new_row)
        grad = grad.at[finish:, start:finish].set(offdiag)
        grad = grad.at[start:finish, start:finish].set(halved_lower(sym))
    return to_stored(grad)
```

```python
import jax
import jax.numpy as jnp
from jax import lax
from jax.sharding import PartitionSpec as P


def product(left, right):
    return jnp.dot(left, right, precision=lax.Precision.HIGH, preferred_element_type=jnp.float32)


def product_tn(left, right):
    return lax.dot_general(
        left,
        right,
        (((0,), (0,)), ((), ())),
        precision=lax.Precision.HIGH,
        preferred_element_type=jnp.float32,
    )


def exact(left, right):
    return jnp.dot(left, right, precision=lax.Precision.HIGHEST, preferred_element_type=jnp.float32)


def halved_lower(matrix):
    return jnp.tril(matrix) - 0.5 * jnp.diag(jnp.diagonal(matrix))


def lower_inverse(tile):
    width = tile.shape[0]
    diag = jnp.diagonal(tile)
    identity = jnp.eye(width, dtype=jnp.float32)
    power = jnp.tril(tile, -1) / diag[:, None]
    total = identity - power
    reach = 2
    while reach < width:
        power = exact(power, power)
        total = total + exact(total, power)
        reach *= 2
    return total / diag[None, :]


def symmetric(inverse_tile, factor_diag, diag_total):
    inner = halved_lower(exact(factor_diag.T, jnp.tril(diag_total)))
    wmat = exact(exact(inverse_tile.T, inner), inverse_tile)
    return wmat + wmat.T


def per_device(factor, adjoint, inverse):
    width = inverse.shape[-1]
    row, col = lax.axis_index("row"), lax.axis_index("col")
    last_row, last_col = lax.axis_size("row") - 1, lax.axis_size("col") - 1
    top, side = factor.shape[0] // 2, factor.shape[1] // 2
    inv_one, inv_two = inverse[0], inverse[1]
    d_one, d_two = lower_inverse(inv_one), lower_inverse(inv_two)

    col_one = jnp.where(col == 0, adjoint[top:, side : side + width], 0.0)
    col_two = jnp.where(col == last_col, adjoint[top:, side - width : side], 0.0)
    row_one = jnp.where(row == 0, factor[top : top + width, :side], 0.0)
    row_two = jnp.where(row == last_row, factor[top - width : top, :side], 0.0)
    corner = jnp.where(
        (row == 0) & (col == last_col), factor[top : top + width, side - width : side], 0.0
    )
    cols = lax.psum(jnp.concatenate([col_one, col_two], 1), "col")
    corner = lax.psum(corner, ("row", "col"))
    rows = lax.psum(jnp.concatenate([row_one, row_two], 0), "row")

    is_top = (jnp.arange(top) < width)[:, None] & (row == 0)
    a_one = jnp.where(is_top, 0.0, product(cols[:, :width], inv_one))
    a_two = jnp.where(is_top, 0.0, product(cols[:, width:] - product(a_one, corner), inv_two))
    both = jnp.concatenate([a_one, a_two], 1)
    lower = factor[top:]
    part = product_tn(both, lower[:, : side + width])
    tile_last = slice(side - width, side)
    diag_one = jnp.where(
        col == 0,
        jnp.where(row == 0, adjoint[top : top + width, side : side + width], 0.0)
        - part[:width, side : side + width],
        0.0,
    )
    edge_one = jnp.where(
        col == last_col,
        jnp.where(row == 0, adjoint[top : top + width, tile_last], 0.0) - part[:width, tile_last],
        0.0,
    )
    diag_two = jnp.where(
        col == last_col,
        jnp.where(row == last_row, adjoint[top - width : top, tile_last], 0.0)
        - part[width:, tile_last],
        0.0,
    )
    tiles = lax.psum(jnp.concatenate([diag_one, edge_one, diag_two], 1), ("row", "col"))
    sums = lax.psum(part[:, :side], "row")

    r_one, r_two = rows[:width], rows[width:]
    left = ((jnp.arange(side) < side - width) | (col != last_col))[None, :]
    r_two = jnp.where(left, r_two, 0.0)
    sym_one = symmetric(inv_one, d_one, tiles[:, :width])
    edge = tiles[:, width : 2 * width] - exact(sym_one, corner)
    a_edge = exact(edge, inv_two)
    diag_total = tiles[:, 2 * width :] - exact(a_edge.T, corner)
    sym_two = symmetric(inv_two, d_two, diag_total)

    new_top = sums[:width] + product(sym_one, r_one)
    a_two = jnp.where(is_top, jnp.pad(a_edge, ((0, top - width), (0, 0))), a_two)
    quad = adjoint[top:, :side] - product(
        jnp.concatenate([a_one, a_two], 1), jnp.concatenate([r_one, r_two], 0)
    )
    quad = quad.at[:width].add(jnp.where(row == 0, -new_top, 0.0))
    quad = quad.at[:, tile_last].set(jnp.where(col == last_col, a_two, quad[:, tile_last]))
    new_row = adjoint[top - width : top, :side] - (
        sums[width:]
        + product(
            jnp.concatenate([a_edge.T, sym_two], 1), jnp.concatenate([r_one, r_two], 0)
        )
    )
    new_row = new_row.at[:, tile_last].set(
        jnp.where(col == last_col, halved_lower(sym_two), new_row[:, tile_last])
    )
    new_row = jnp.where(row == last_row, new_row, adjoint[top - width : top, :side])
    new_col = a_one.at[:width].set(jnp.where(row == 0, halved_lower(sym_one), a_one[:width]))
    new_col = jnp.where(col == 0, new_col, adjoint[top:, side : side + width])
    out = adjoint.at[top:, :side].set(quad)
    out = out.at[top - width : top, :side].set(new_row)
    return out.at[top:, side : side + width].set(new_col)


def solution(mesh):
    return jax.shard_map(
        per_device,
        mesh=mesh,
        in_specs=(P("row", "col"), P("row", "col"), P()),
        out_specs=P("row", "col"),
        check_vma=False,
    )
```

```python
import functools

import jax
import jax.numpy as jnp
from jax import lax
from jax.experimental import pallas as pl
from jax.experimental.pallas import tpu as pltpu
from jax.sharding import PartitionSpec as P

F32 = jnp.float32
MESH = pl.DeviceIdType.MESH
SLOTS = 10
COL_CHUNKS = 4
CORNER_CHUNKS = 4
ROW_CHUNKS = 8
CRIT_CHUNKS = 2


def split(value):
    high = value.astype(jnp.bfloat16)
    return high, (value - high.astype(F32)).astype(jnp.bfloat16)


def product(left, right):
    left_high, left_low = split(left)
    right_high, right_low = split(right)
    dot = functools.partial(jnp.dot, preferred_element_type=F32)
    return dot(left_high, right_high) + (dot(left_high, right_low) + dot(left_low, right_high))


def exact(left, right):
    return jnp.dot(left, right, precision=lax.Precision.HIGHEST, preferred_element_type=F32)


def iotas(width):
    rows = lax.broadcasted_iota(jnp.int32, (width, width), 0)
    cols = lax.broadcasted_iota(jnp.int32, (width, width), 1)
    return rows, cols


def halved_lower(matrix):
    rows, cols = iotas(matrix.shape[0])
    return jnp.where(rows > cols, matrix, jnp.where(rows == cols, 0.5 * matrix, 0.0))


def lower_inverse(tile):
    width = tile.shape[0]
    rows, cols = iotas(width)
    diagonal = jnp.where(rows == cols, tile, 0.0)
    power = jnp.where(rows > cols, tile, 0.0) / jnp.sum(diagonal, axis=1, keepdims=True)
    total = jnp.where(rows == cols, 1.0, 0.0) - power
    reach = 2
    while reach < width:
        power = exact(power, power)
        total = total + exact(total, power)
        reach *= 2
    return total / jnp.sum(diagonal, axis=0, keepdims=True)


def symmetric(inverse_tile, factor_diag, diag_total):
    rows, cols = iotas(inverse_tile.shape[0])
    inner = halved_lower(exact(factor_diag.T, jnp.where(rows >= cols, diag_total, 0.0)))
    wmat = exact(exact(inverse_tile.T, inner), inverse_tile)
    return wmat + wmat.T


class Line:
    def __init__(self, axis):
        self.axis = axis
        self.count = lax.axis_size(axis)
        self.place = lax.axis_index(axis)
        self.mine = lax.rem(self.place, 2)
        step = 2 - 4 * self.mine
        self.partner = self.place + 1 - 2 * self.mine
        self.prev = self.place - step
        self.next = self.place + step
        self.first = self.place == self.mine * (self.count - 1)
        self.last = self.place == (self.count - 2) * (1 - self.mine) + self.mine


def row_kernel(
    factor, adjoint, inverse, a_out, r_out, fix_out, phi_out,
    lower, cols, offdiag, rows_buf, corner, part, from_partner, from_next, crit, ldiag,
    edge_in, edge_own, dmat, local_sem, load_sem,
    cols_recv, cols_send, corner_crecv, corner_csend, corner_rrecv, corner_rsend,
    rows_recv, rows_send, leaf_send, chain_send, partner_recv, next_recv,
    crit_recv, crit_send, edge_sems, out_sem,
):
    width = inverse.shape[-1]
    half = width // 2
    top, side = cols.shape[1], rows_buf.shape[2]
    row, col = Line("row"), Line("col")
    top_row, bottom_row = row.place == 0, row.place == row.count - 1
    end_row = top_row | bottom_row

    def remote(src, dst, send, recv, line, target):
        return pltpu.make_async_remote_copy(
            src_ref=src, dst_ref=dst, send_sem=send, recv_sem=recv,
            device_id={line.axis: target}, device_id_type=MESH,
        )

    barrier = pltpu.get_barrier_semaphore()
    for line in (row, col):
        pl.semaphore_signal(barrier, inc=1, device_id={line.axis: line.partner}, device_id_type=MESH)

        @pl.when(jnp.logical_not(line.first))
        def _():
            pl.semaphore_signal(barrier, inc=1, device_id={line.axis: line.prev}, device_id_type=MESH)

        @pl.when(jnp.logical_not(line.last))
        def _():
            pl.semaphore_signal(barrier, inc=1, device_id={line.axis: line.next}, device_id_type=MESH)

    @pl.when(end_row)
    def _():
        pl.semaphore_signal(
            barrier, inc=1, device_id={"row": row.count - 1 - row.place}, device_id_type=MESH
        )

    lower_load = pltpu.make_async_copy(
        factor.at[pl.ds(top, top), pl.ds(0, side + width)], lower, load_sem
    )
    lower_load.start()
    panel_start = side - width * col.mine
    row_start = top - width * row.mine

    @pl.when(col.first)
    def _():
        copy = pltpu.make_async_copy(
            adjoint.at[pl.ds(top, top), pl.ds(pl.multiple_of(panel_start, width), width)],
            cols.at[col.mine], local_sem.at[0],
        )
        copy.start()
        copy.wait()

    @pl.when(top_row & (col.place == col.count - 1))
    def _():
        copy = pltpu.make_async_copy(
            factor.at[pl.ds(top, width), pl.ds(side - width, width)], corner, local_sem.at[1]
        )
        copy.start()
        copy.wait()

    @pl.when(row.first)
    def _():
        copy = pltpu.make_async_copy(
            factor.at[pl.ds(pl.multiple_of(row_start, width), width), pl.ds(0, side)],
            rows_buf.at[row.mine], local_sem.at[2],
        )
        copy.start()
        copy.wait()

    @pl.when(bottom_row)
    def _():
        copy = pltpu.make_async_copy(
            adjoint.at[pl.ds(top - width, width), pl.ds(side - width, width)], ldiag, local_sem.at[3]
        )
        copy.start()
        copy.wait()

    expected = 2 + sum(
        jnp.where(line.first, 0, 1) + jnp.where(line.last, 0, 1) for line in (row, col)
    )
    pl.semaphore_wait(barrier, expected + jnp.where(end_row, 1, 0))

    def pass_on(line, buf, size, chunk, recv, send, panel=None):
        lead = line.mine if panel is None else panel
        ref = buf.at[lead, pl.ds(pl.multiple_of(chunk * size, 8), size)]

        @pl.when(jnp.logical_not(line.first))
        def _():
            remote(ref, ref, send.at[0, chunk], recv.at[lead, chunk], line, line.partner).wait_recv()

        @pl.when(jnp.logical_not(line.last))
        def _():
            remote(ref, ref, send.at[0, chunk], recv.at[lead, chunk], line, line.next).start()

        remote(ref, ref, send.at[1, chunk], recv.at[lead, chunk], line, line.partner).start()

    def take(line, buf, size, chunk, recv, send):
        lead = 1 - line.mine
        ref = buf.at[lead, pl.ds(pl.multiple_of(chunk * size, 8), size)]
        remote(ref, ref, send.at[1, chunk], recv.at[lead, chunk], line, line.partner).wait_recv()

    def finish_sends(line, buf, size, chunks, send, recv):
        def body(chunk, carry):
            ref = buf.at[line.mine, pl.ds(pl.multiple_of(chunk * size, 8), size)]

            @pl.when(jnp.logical_not(line.last))
            def _():
                remote(ref, ref, send.at[0, chunk], recv.at[0, chunk], line, line.next).wait_send()

            remote(ref, ref, send.at[1, chunk], recv.at[0, chunk], line, line.partner).wait_send()
            return carry

        lax.fori_loop(0, chunks, body, 0)

    def loop(start, stop, step):
        def body(index, carry):
            step(index)
            return carry

        lax.fori_loop(start, stop, body, 0)

    cols_size = top // COL_CHUNKS
    rows_size = width // ROW_CHUNKS
    corner_size = width // CORNER_CHUNKS
    loop(0, COL_CHUNKS, lambda c: pass_on(col, cols, cols_size, c, cols_recv, cols_send))

    def corner_ref(chunk):
        return corner.at[pl.ds(pl.multiple_of(chunk * corner_size, 8), corner_size)]

    def corner_cols(chunk):
        ref = corner_ref(chunk)

        @pl.when(col.mine == 1)
        def _():
            @pl.when(jnp.logical_not(col.first))
            def _():
                remote(
                    ref, ref, corner_csend.at[0, chunk], corner_crecv.at[chunk], col, col.partner
                ).wait_recv()

            @pl.when(jnp.logical_not(col.last))
            def _():
                remote(
                    ref, ref, corner_csend.at[0, chunk], corner_crecv.at[chunk], col, col.next
                ).start()

            remote(
                ref, ref, corner_csend.at[1, chunk], corner_crecv.at[chunk], col, col.partner
            ).start()

        @pl.when(col.mine == 0)
        def _():
            remote(
                ref, ref, corner_csend.at[1, chunk], corner_crecv.at[chunk], col, col.partner
            ).wait_recv()

    def corner_rows(chunk):
        ref = corner_ref(chunk)

        @pl.when(jnp.logical_not(top_row))
        def _():
            remote(
                ref, ref, corner_rsend.at[0, chunk], corner_rrecv.at[chunk], row, row.partner
            ).wait_recv()

        @pl.when(row.mine == 0)
        def _():
            @pl.when(jnp.logical_not(row.last))
            def _():
                remote(
                    ref, ref, corner_rsend.at[0, chunk], corner_rrecv.at[chunk], row, row.next
                ).start()

            remote(
                ref, ref, corner_rsend.at[1, chunk], corner_rrecv.at[chunk], row, row.partner
            ).start()

    def corner_step(chunk):
        @pl.when(top_row)
        def _():
            corner_cols(chunk)

        corner_rows(chunk)

    @pl.when(top_row)
    def _():
        loop(0, CORNER_CHUNKS, corner_step)

    @pl.when(row.first)
    def _():
        loop(0, ROW_CHUNKS, lambda c: pass_on(row, rows_buf, rows_size, c, rows_recv, rows_send))

    loop(0, COL_CHUNKS, lambda c: take(col, cols, cols_size, c, cols_recv, cols_send))
    lower_load.wait()

    def own_terms(panel, first_slot):
        left = offdiag[panel].T
        left_high, left_low = split(left)
        dot = functools.partial(jnp.dot, preferred_element_type=F32)

        def body(tile, carry):
            start = jnp.where(tile == 0, side, jnp.where(tile == 1, side - width, (tile - 2) * width))
            right = lower[:, pl.ds(pl.multiple_of(start, width), width)]
            high, low = split(right)
            value = dot(left_high, high) + (dot(left_high, low) + dot(left_low, high))
            part[panel, 2 * tile] = value[:half]
            part[panel, 2 * tile + 1] = value[half:]
            return carry

        lax.fori_loop(first_slot // 2, SLOTS // 2, body, 0)

        @pl.when(row.mine == 1 - panel)
        def _():
            send_start = jnp.where((col.place == 0) & (panel == 0), 0, 2)
            loop(
                send_start, SLOTS,
                lambda s: remote(
                    part.at[panel, s], from_partner.at[s], leaf_send.at[s], partner_recv.at[s],
                    row, row.partner,
                ).start(),
            )

    offdiag[0] = product(cols[0], inverse[0])

    @pl.when(top_row)
    def _():
        offdiag[0, :width] = jnp.zeros((width, width), F32)

    own_terms(0, 0)

    @pl.when(jnp.logical_not(top_row))
    def _():
        loop(0, CORNER_CHUNKS, corner_step)

    offdiag[1] = product(cols[1] - product(offdiag[0], corner[...]), inverse[1])

    @pl.when(top_row)
    def _():
        offdiag[1, :width] = jnp.zeros((width, width), F32)

    own_terms(1, 2)

    @pl.when(end_row)
    def _():
        dmat[...] = lower_inverse(inverse[row.mine])

    slot_start = jnp.where((col.place == 0) & (row.mine == 0), 0, 2)

    def reduce_step(slot):
        mine = part.at[row.mine, slot]
        remote(
            mine, from_partner.at[slot], leaf_send.at[slot], partner_recv.at[slot], row, row.partner
        ).wait_recv()
        part[row.mine, slot] = part[row.mine, slot] + from_partner[slot]

        @pl.when(jnp.logical_not(row.last))
        def _():
            remote(
                mine, from_next.at[slot], chain_send.at[slot], next_recv.at[slot], row, row.partner
            ).wait_recv()
            part[row.mine, slot] = part[row.mine, slot] + from_next[slot]

        @pl.when(jnp.logical_not(row.first))
        def _():
            remote(
                mine, from_next.at[slot], chain_send.at[slot], next_recv.at[slot], row, row.prev
            ).start()

    def stream_step(index):
        @pl.when((index < ROW_CHUNKS) & jnp.logical_not(row.first))
        def _():
            pass_on(row, rows_buf, rows_size, index, rows_recv, rows_send)

        @pl.when(index >= slot_start)
        def _():
            reduce_step(index)

    loop(0, 4, stream_step)
    crit_size = width // CRIT_CHUNKS

    @pl.when(end_row)
    def _():
        @pl.when(col.first)
        def _():
            lead = col.mine
            slot = 2 * jnp.maximum(lead, row.mine)
            for piece in range(2):
                span = slice(half * piece, half * (piece + 1))
                value = part[row.mine, slot + piece]
                crit[lead, span] = jnp.where(bottom_row, ldiag[span] - value, value)

        loop(0, CRIT_CHUNKS, lambda c: pass_on(col, crit, crit_size, c, crit_recv, crit_send))
        loop(0, CRIT_CHUNKS, lambda c: take(col, crit, crit_size, c, crit_recv, crit_send))

    def edge_copy():
        return remote(
            edge_own, edge_in, edge_sems.at[0], edge_sems.at[1], row, row.count - 1
        )

    @pl.when(top_row)
    def _():
        sym = symmetric(inverse[0], dmat[...], cols[0, :width] - crit[0])
        edge_own[...] = product(cols[1, :width] - crit[1] - product(sym, corner[...]), inverse[1])
        edge_copy().start()
        offdiag[1, :width] = edge_own[...]
        dmat[...] = sym

    loop(4, SLOTS, stream_step)
    loop(0, ROW_CHUNKS, lambda c: take(row, rows_buf, rows_size, c, rows_recv, rows_send))

    outs = [
        pltpu.make_async_copy(offdiag, a_out, out_sem.at[0]),
        pltpu.make_async_copy(rows_buf, r_out, out_sem.at[1]),
    ]
    for copy in outs:
        copy.start()

    @pl.when(bottom_row)
    def _():
        edge_copy().wait_recv()
        edge_t = edge_in[...].T
        edge_own[...] = edge_t
        diag_total = crit[1] - product(edge_t, corner[...])
        dmat[...] = symmetric(inverse[1], dmat[...], diag_total)

    @pl.when(end_row)
    def _():
        phi_out[...] = halved_lower(dmat[...])

        def body(tile, carry):
            slot = jnp.where(tile == side // width - 1, 2, 2 * tile + 4)
            start = pl.multiple_of(tile * width, width)
            value = product(dmat[...], rows_buf[row.mine, :, pl.ds(start, width)])
            fix_out[:half, pl.ds(start, width)] = value[:half] + part[row.mine, slot]
            fix_out[half:, pl.ds(start, width)] = value[half:] + part[row.mine, slot + 1]

            @pl.when(bottom_row)
            def _():
                fix_out[:, pl.ds(start, width)] = fix_out[:, pl.ds(start, width)] + product(
                    edge_own[...], rows_buf[0, :, pl.ds(start, width)]
                )

            return carry

        lax.fori_loop(0, side // width, body, 0)

    finish_sends(col, cols, cols_size, COL_CHUNKS, cols_send, cols_recv)
    finish_sends(row, rows_buf, rows_size, ROW_CHUNKS, rows_send, rows_recv)

    @pl.when(end_row)
    def _():
        finish_sends(col, crit, crit_size, CRIT_CHUNKS, crit_send, crit_recv)

    def corner_finish(chunk):
        ref = corner_ref(chunk)

        @pl.when(top_row & (col.mine == 1))
        def _():
            @pl.when(jnp.logical_not(col.last))
            def _():
                remote(
                    ref, ref, corner_csend.at[0, chunk], corner_crecv.at[chunk], col, col.next
                ).wait_send()

            remote(
                ref, ref, corner_csend.at[1, chunk], corner_crecv.at[chunk], col, col.partner
            ).wait_send()

        @pl.when(row.mine == 0)
        def _():
            @pl.when(jnp.logical_not(row.last))
            def _():
                remote(
                    ref, ref, corner_rsend.at[0, chunk], corner_rrecv.at[chunk], row, row.next
                ).wait_send()

            remote(
                ref, ref, corner_rsend.at[1, chunk], corner_rrecv.at[chunk], row, row.partner
            ).wait_send()

    loop(0, CORNER_CHUNKS, corner_finish)
    leaf_start = jnp.where((col.place == 0) & (row.mine == 1), 0, 2)
    loop(
        leaf_start, SLOTS,
        lambda s: remote(
            part.at[1 - row.mine, s], from_partner.at[s], leaf_send.at[s], partner_recv.at[s],
            row, row.partner,
        ).wait_send(),
    )

    @pl.when(jnp.logical_not(row.first))
    def _():
        loop(
            slot_start, SLOTS,
            lambda s: remote(
                part.at[row.mine, s], from_next.at[s], chain_send.at[s], next_recv.at[s],
                row, row.prev,
            ).wait_send(),
        )

    @pl.when(top_row)
    def _():
        edge_copy().wait_send()

    for copy in outs:
        copy.wait()


def update_kernel(adjoint, offdiag, rows, fix, phi, out):
    step = pl.program_id(0)
    middle = pl.num_programs(0) // 2
    width, side = phi.shape[0], fix.shape[1]
    top_row = lax.axis_index("row") == 0
    bottom_row = lax.axis_index("row") == lax.axis_size("row") - 1
    first_col = lax.axis_index("col") == 0
    last_col = lax.axis_index("col") == lax.axis_size("col") - 1
    out[...] = adjoint[...]

    @pl.when(step >= middle)
    def _():
        pairs = [split(offdiag[panel]) for panel in range(2)]
        dot = functools.partial(jnp.dot, preferred_element_type=F32)

        for start in range(0, side, width):
            value = adjoint[:, start : start + width]
            for panel, (left_high, left_low) in enumerate(pairs):
                high, low = split(rows[panel, :, start : start + width])
                value -= dot(left_high, high) + (dot(left_high, low) + dot(left_low, high))
            out[:, start : start + width] = value

        @pl.when(top_row & (step == middle))
        def _():
            out[:, :side] = out[:, :side] - fix[...]

        @pl.when(last_col)
        def _():
            out[:, side - width : side] = offdiag[1]

        @pl.when(first_col)
        def _():
            out[:, side : side + width] = offdiag[0]

            @pl.when(top_row & (step == middle))
            def _():
                out[:, side : side + width] = phi[...]

    @pl.when(bottom_row & (step == middle - 1))
    def _():
        out[:, :side] = adjoint[:, :side] - fix[...]

        @pl.when(last_col)
        def _():
            out[:, side - width : side] = phi[...]


def per_device(factor, adjoint, inverse):
    width = inverse.shape[-1]
    height, total = factor.shape
    top, side = height // 2, total // 2
    half = width // 2
    any_spec = pl.BlockSpec(memory_space=pl.ANY)
    vmem_spec = pl.BlockSpec(memory_space=pltpu.VMEM)
    dma = pltpu.SemaphoreType.DMA
    offdiag, rows, fix, phi = pl.pallas_call(
        row_kernel,
        out_shape=[
            jax.ShapeDtypeStruct((2, top, width), F32),
            jax.ShapeDtypeStruct((2, width, side), F32),
            jax.ShapeDtypeStruct((width, side), F32),
            jax.ShapeDtypeStruct((width, width), F32),
        ],
        in_specs=[any_spec, any_spec, vmem_spec],
        out_specs=[any_spec, any_spec, vmem_spec, vmem_spec],
        scratch_shapes=[
            pltpu.VMEM((top, side + width), F32),
            pltpu.VMEM((2, top, width), F32),
            pltpu.VMEM((2, top, width), F32),
            pltpu.VMEM((2, width, side), F32),
            pltpu.VMEM((width, width), F32),
            pltpu.VMEM((2, SLOTS, half, width), F32),
            pltpu.VMEM((SLOTS, half, width), F32),
            pltpu.VMEM((SLOTS, half, width), F32),
            pltpu.VMEM((2, width, width), F32),
            pltpu.VMEM((width, width), F32),
            pltpu.VMEM((width, width), F32),
            pltpu.VMEM((width, width), F32),
            pltpu.VMEM((width, width), F32),
            dma((4,)),
            dma,
            dma((2, COL_CHUNKS)),
            dma((2, COL_CHUNKS)),
            dma((CORNER_CHUNKS,)),
            dma((2, CORNER_CHUNKS)),
            dma((CORNER_CHUNKS,)),
            dma((2, CORNER_CHUNKS)),
            dma((2, ROW_CHUNKS)),
            dma((2, ROW_CHUNKS)),
            dma((SLOTS,)),
            dma((SLOTS,)),
            dma((SLOTS,)),
            dma((SLOTS,)),
            dma((2, CRIT_CHUNKS)),
            dma((2, CRIT_CHUNKS)),
            dma((2,)),
            dma((2,)),
        ],
        compiler_params=pltpu.CompilerParams(
            collective_id=0, has_side_effects=True, vmem_limit_bytes=40 * 2**20
        ),
        name="panels",
    )(factor, adjoint, inverse)
    steps = height // width
    middle = steps // 2
    return pl.pallas_call(
        update_kernel,
        grid=(steps,),
        out_shape=jax.ShapeDtypeStruct(adjoint.shape, F32),
        in_specs=[
            pl.BlockSpec((width, total), lambda t: (t, 0)),
            pl.BlockSpec((2, width, width), lambda t: (0, jnp.maximum(t - middle, 0), 0)),
            pl.BlockSpec((2, width, side), lambda t: (0, 0, 0)),
            pl.BlockSpec((width, side), lambda t: (0, 0)),
            pl.BlockSpec((width, width), lambda t: (0, 0)),
        ],
        out_specs=pl.BlockSpec((width, total), lambda t: (t, 0)),
        compiler_params=pltpu.CompilerParams(vmem_limit_bytes=40 * 2**20),
        name="update",
    )(adjoint, offdiag, rows, fix, phi)


def solution(mesh):
    return jax.shard_map(
        per_device,
        mesh=mesh,
        in_specs=(P("row", "col"), P("row", "col"), P()),
        out_specs=P("row", "col"),
        check_vma=False,
    )
```

```python
import functools

import jax
import jax.numpy as jnp
from jax import lax
from jax.experimental import pallas as pl
from jax.experimental.pallas import tpu as pltpu
from jax.sharding import PartitionSpec as P

F32 = jnp.float32
MESH = pl.DeviceIdType.MESH
SLOTS = 10
COL_CHUNKS = 4
CORNER_CHUNKS = 4
ROW_CHUNKS = 8
CRIT_CHUNKS = 2


def split(value):
    high = value.astype(jnp.bfloat16)
    return high, (value - high.astype(F32)).astype(jnp.bfloat16)


def product(left, right):
    left_high, left_low = split(left)
    right_high, right_low = split(right)
    dot = functools.partial(jnp.dot, preferred_element_type=F32)
    return dot(left_high, right_high) + (dot(left_high, right_low) + dot(left_low, right_high))


def exact(left, right):
    return jnp.dot(left, right, precision=lax.Precision.HIGHEST, preferred_element_type=F32)


def iotas(width):
    rows = lax.broadcasted_iota(jnp.int32, (width, width), 0)
    cols = lax.broadcasted_iota(jnp.int32, (width, width), 1)
    return rows, cols


def halved_lower(matrix):
    rows, cols = iotas(matrix.shape[0])
    return jnp.where(rows > cols, matrix, jnp.where(rows == cols, 0.5 * matrix, 0.0))


def lower_inverse(tile):
    width = tile.shape[0]
    rows, cols = iotas(width)
    diagonal = jnp.where(rows == cols, tile, 0.0)
    power = jnp.where(rows > cols, tile, 0.0) / jnp.sum(diagonal, axis=1, keepdims=True)
    total = jnp.where(rows == cols, 1.0, 0.0) - power
    reach = 2
    while reach < width:
        power = exact(power, power)
        total = total + exact(total, power)
        reach *= 2
    return total / jnp.sum(diagonal, axis=0, keepdims=True)


def symmetric(inverse_tile, factor_diag, diag_total):
    rows, cols = iotas(inverse_tile.shape[0])
    inner = halved_lower(exact(factor_diag.T, jnp.where(rows >= cols, diag_total, 0.0)))
    wmat = exact(exact(inverse_tile.T, inner), inverse_tile)
    return wmat + wmat.T


class Line:
    def __init__(self, axis):
        self.axis = axis
        self.count = lax.axis_size(axis)
        self.place = lax.axis_index(axis)
        self.mine = lax.rem(self.place, 2)
        step = 2 - 4 * self.mine
        self.partner = self.place + 1 - 2 * self.mine
        self.prev = self.place - step
        self.next = self.place + step
        self.first = self.place == self.mine * (self.count - 1)
        self.last = self.place == (self.count - 2) * (1 - self.mine) + self.mine


def row_kernel(
    factor, adjoint, inverse, a_out, r_out, fix_out, phi_out,
    lower, cols, offdiag, rows_buf, corner, part, from_partner, from_next, crit, ldiag,
    edge_in, edge_own, dmat, local_sem, load_sem,
    cols_recv, cols_send, corner_crecv, corner_csend, corner_rrecv, corner_rsend,
    rows_recv, rows_send, leaf_send, chain_send, partner_recv, next_recv,
    crit_recv, crit_send, edge_sems, out_sem,
):
    width = inverse.shape[-1]
    half = width // 2
    top, side = cols.shape[1], rows_buf.shape[2]
    row, col = Line("row"), Line("col")
    top_row, bottom_row = row.place == 0, row.place == row.count - 1
    end_row = top_row | bottom_row

    def remote(src, dst, send, recv, line, target):
        return pltpu.make_async_remote_copy(
            src_ref=src, dst_ref=dst, send_sem=send, recv_sem=recv,
            device_id={line.axis: target}, device_id_type=MESH,
        )

    barrier = pltpu.get_barrier_semaphore()
    for line in (row, col):
        pl.semaphore_signal(barrier, inc=1, device_id={line.axis: line.partner}, device_id_type=MESH)

        @pl.when(jnp.logical_not(line.first))
        def _():
            pl.semaphore_signal(barrier, inc=1, device_id={line.axis: line.prev}, device_id_type=MESH)

        @pl.when(jnp.logical_not(line.last))
        def _():
            pl.semaphore_signal(barrier, inc=1, device_id={line.axis: line.next}, device_id_type=MESH)

    @pl.when(end_row)
    def _():
        pl.semaphore_signal(
            barrier, inc=1, device_id={"row": row.count - 1 - row.place}, device_id_type=MESH
        )

    lower_load = pltpu.make_async_copy(
        factor.at[pl.ds(top, top), pl.ds(0, side + width)], lower, load_sem
    )
    lower_load.start()
    panel_start = side - width * col.mine
    row_start = top - width * row.mine

    @pl.when(col.first)
    def _():
        copy = pltpu.make_async_copy(
            adjoint.at[pl.ds(top, top), pl.ds(pl.multiple_of(panel_start, width), width)],
            cols.at[col.mine], local_sem.at[0],
        )
        copy.start()
        copy.wait()

    @pl.when(top_row & (col.place == col.count - 1))
    def _():
        copy = pltpu.make_async_copy(
            factor.at[pl.ds(top, width), pl.ds(side - width, width)], corner, local_sem.at[1]
        )
        copy.start()
        copy.wait()

    @pl.when(row.first)
    def _():
        copy = pltpu.make_async_copy(
            factor.at[pl.ds(pl.multiple_of(row_start, width), width), pl.ds(0, side)],
            rows_buf.at[row.mine], local_sem.at[2],
        )
        copy.start()
        copy.wait()

    @pl.when(bottom_row)
    def _():
        copy = pltpu.make_async_copy(
            adjoint.at[pl.ds(top - width, width), pl.ds(side - width, width)], ldiag, local_sem.at[3]
        )
        copy.start()
        copy.wait()

    expected = 2 + sum(
        jnp.where(line.first, 0, 1) + jnp.where(line.last, 0, 1) for line in (row, col)
    )
    pl.semaphore_wait(barrier, expected + jnp.where(end_row, 1, 0))

    def pass_on(line, buf, size, chunk, recv, send, panel=None):
        lead = line.mine if panel is None else panel
        ref = buf.at[lead, pl.ds(pl.multiple_of(chunk * size, 8), size)]

        @pl.when(jnp.logical_not(line.first))
        def _():
            remote(ref, ref, send.at[0, chunk], recv.at[lead, chunk], line, line.partner).wait_recv()

        @pl.when(jnp.logical_not(line.last))
        def _():
            remote(ref, ref, send.at[0, chunk], recv.at[lead, chunk], line, line.next).start()

        remote(ref, ref, send.at[1, chunk], recv.at[lead, chunk], line, line.partner).start()

    def take(line, buf, size, chunk, recv, send):
        lead = 1 - line.mine
        ref = buf.at[lead, pl.ds(pl.multiple_of(chunk * size, 8), size)]
        remote(ref, ref, send.at[1, chunk], recv.at[lead, chunk], line, line.partner).wait_recv()

    def finish_sends(line, buf, size, chunks, send, recv):
        def body(chunk, carry):
            ref = buf.at[line.mine, pl.ds(pl.multiple_of(chunk * size, 8), size)]

            @pl.when(jnp.logical_not(line.last))
            def _():
                remote(ref, ref, send.at[0, chunk], recv.at[0, chunk], line, line.next).wait_send()

            remote(ref, ref, send.at[1, chunk], recv.at[0, chunk], line, line.partner).wait_send()
            return carry

        lax.fori_loop(0, chunks, body, 0)

    def loop(start, stop, step):
        def body(index, carry):
            step(index)
            return carry

        lax.fori_loop(start, stop, body, 0)

    cols_size = top // COL_CHUNKS
    rows_size = width // ROW_CHUNKS
    corner_size = width // CORNER_CHUNKS
    loop(0, COL_CHUNKS, lambda c: pass_on(col, cols, cols_size, c, cols_recv, cols_send))

    def corner_ref(chunk):
        return corner.at[pl.ds(pl.multiple_of(chunk * corner_size, 8), corner_size)]

    def corner_cols(chunk):
        ref = corner_ref(chunk)

        @pl.when(col.mine == 1)
        def _():
            @pl.when(jnp.logical_not(col.first))
            def _():
                remote(
                    ref, ref, corner_csend.at[0, chunk], corner_crecv.at[chunk], col, col.partner
                ).wait_recv()

            @pl.when(jnp.logical_not(col.last))
            def _():
                remote(
                    ref, ref, corner_csend.at[0, chunk], corner_crecv.at[chunk], col, col.next
                ).start()

            remote(
                ref, ref, corner_csend.at[1, chunk], corner_crecv.at[chunk], col, col.partner
            ).start()

        @pl.when(col.mine == 0)
        def _():
            remote(
                ref, ref, corner_csend.at[1, chunk], corner_crecv.at[chunk], col, col.partner
            ).wait_recv()

    def corner_rows(chunk):
        ref = corner_ref(chunk)

        @pl.when(jnp.logical_not(top_row))
        def _():
            remote(
                ref, ref, corner_rsend.at[0, chunk], corner_rrecv.at[chunk], row, row.partner
            ).wait_recv()

        @pl.when(row.mine == 0)
        def _():
            @pl.when(jnp.logical_not(row.last))
            def _():
                remote(
                    ref, ref, corner_rsend.at[0, chunk], corner_rrecv.at[chunk], row, row.next
                ).start()

            remote(
                ref, ref, corner_rsend.at[1, chunk], corner_rrecv.at[chunk], row, row.partner
            ).start()

    def corner_step(chunk):
        @pl.when(top_row)
        def _():
            corner_cols(chunk)

        corner_rows(chunk)

    @pl.when(top_row)
    def _():
        loop(0, CORNER_CHUNKS, corner_step)

    @pl.when(row.first)
    def _():
        loop(0, ROW_CHUNKS, lambda c: pass_on(row, rows_buf, rows_size, c, rows_recv, rows_send))

    loop(0, COL_CHUNKS, lambda c: take(col, cols, cols_size, c, cols_recv, cols_send))
    lower_load.wait()

    def leaf_copy(panel, slot):
        return remote(
            part.at[panel, slot], from_partner.at[slot], leaf_send.at[slot], partner_recv.at[slot],
            row, row.partner,
        )

    def own_terms(panel, first_tile, between):
        left_high, left_low = split(offdiag[panel].T)
        dot = functools.partial(jnp.dot, preferred_element_type=F32)

        def body(tile, carry):
            start = jnp.where(tile == 0, side, jnp.where(tile == 1, side - width, (tile - 2) * width))
            right = lower[:, pl.ds(pl.multiple_of(start, width), width)]
            high, low = split(right)
            value = dot(left_high, high) + (dot(left_high, low) + dot(left_low, high))
            part[panel, 2 * tile] = value[:half]
            part[panel, 2 * tile + 1] = value[half:]
            wanted = row.mine == 1 - panel
            if panel == 0:
                wanted = wanted & ((tile > 0) | (col.place == 0))

            @pl.when(wanted)
            def _():
                leaf_copy(panel, 2 * tile).start()
                leaf_copy(panel, 2 * tile + 1).start()

            between(tile)
            return carry

        lax.fori_loop(first_tile, SLOTS // 2, body, 0)

    def pass_rows(chunk):
        @pl.when((chunk < ROW_CHUNKS) & jnp.logical_not(row.first))
        def _():
            pass_on(row, rows_buf, rows_size, chunk, rows_recv, rows_send)

    def between_one(tile):
        @pl.when((tile < CORNER_CHUNKS) & jnp.logical_not(top_row))
        def _():
            corner_step(tile)

        pass_rows(tile)

    offdiag[0] = product(cols[0], inverse[0])

    @pl.when(top_row)
    def _():
        offdiag[0, :width] = jnp.zeros((width, width), F32)

    own_terms(0, 0, between_one)
    offdiag[1] = product(cols[1] - product(offdiag[0], corner[...]), inverse[1])

    @pl.when(top_row)
    def _():
        offdiag[1, :width] = jnp.zeros((width, width), F32)

    own_terms(1, 1, lambda tile: pass_rows(SLOTS // 2 - 1 + tile))
    loop(SLOTS - 1, ROW_CHUNKS, pass_rows)

    @pl.when(end_row)
    def _():
        dmat[...] = lower_inverse(inverse[row.mine])

    slot_start = jnp.where((col.place == 0) & (row.mine == 0), 0, 2)

    def reduce_step(slot):
        mine = part.at[row.mine, slot]
        remote(
            mine, from_partner.at[slot], leaf_send.at[slot], partner_recv.at[slot], row, row.partner
        ).wait_recv()
        part[row.mine, slot] = part[row.mine, slot] + from_partner[slot]

        @pl.when(jnp.logical_not(row.last))
        def _():
            remote(
                mine, from_next.at[slot], chain_send.at[slot], next_recv.at[slot], row, row.partner
            ).wait_recv()
            part[row.mine, slot] = part[row.mine, slot] + from_next[slot]

        @pl.when(jnp.logical_not(row.first))
        def _():
            remote(
                mine, from_next.at[slot], chain_send.at[slot], next_recv.at[slot], row, row.prev
            ).start()

    loop(slot_start, 4, reduce_step)
    crit_size = width // CRIT_CHUNKS

    @pl.when(end_row)
    def _():
        @pl.when(col.first)
        def _():
            lead = col.mine
            slot = 2 * jnp.maximum(lead, row.mine)
            for piece in range(2):
                span = slice(half * piece, half * (piece + 1))
                value = part[row.mine, slot + piece]
                crit[lead, span] = jnp.where(bottom_row, ldiag[span] - value, value)

        loop(0, CRIT_CHUNKS, lambda c: pass_on(col, crit, crit_size, c, crit_recv, crit_send))
        loop(0, CRIT_CHUNKS, lambda c: take(col, crit, crit_size, c, crit_recv, crit_send))

    def edge_copy():
        return remote(
            edge_own, edge_in, edge_sems.at[0], edge_sems.at[1], row, row.count - 1
        )

    @pl.when(top_row)
    def _():
        sym = symmetric(inverse[0], dmat[...], cols[0, :width] - crit[0])
        edge_own[...] = product(cols[1, :width] - crit[1] - product(sym, corner[...]), inverse[1])
        edge_copy().start()
        offdiag[1, :width] = edge_own[...]
        dmat[...] = sym

    loop(4, SLOTS, reduce_step)
    loop(0, ROW_CHUNKS, lambda c: take(row, rows_buf, rows_size, c, rows_recv, rows_send))

    outs = [
        pltpu.make_async_copy(offdiag, a_out, out_sem.at[0]),
        pltpu.make_async_copy(rows_buf, r_out, out_sem.at[1]),
    ]
    for copy in outs:
        copy.start()

    @pl.when(bottom_row)
    def _():
        edge_copy().wait_recv()
        edge_t = edge_in[...].T
        edge_own[...] = edge_t
        diag_total = crit[1] - product(edge_t, corner[...])
        dmat[...] = symmetric(inverse[1], dmat[...], diag_total)

    @pl.when(end_row)
    def _():
        phi_out[...] = halved_lower(dmat[...])

        def body(tile, carry):
            slot = jnp.where(tile == side // width - 1, 2, 2 * tile + 4)
            start = pl.multiple_of(tile * width, width)
            value = product(dmat[...], rows_buf[row.mine, :, pl.ds(start, width)])
            fix_out[:half, pl.ds(start, width)] = value[:half] + part[row.mine, slot]
            fix_out[half:, pl.ds(start, width)] = value[half:] + part[row.mine, slot + 1]

            @pl.when(bottom_row)
            def _():
                fix_out[:, pl.ds(start, width)] = fix_out[:, pl.ds(start, width)] + product(
                    edge_own[...], rows_buf[0, :, pl.ds(start, width)]
                )

            return carry

        lax.fori_loop(0, side // width, body, 0)

    finish_sends(col, cols, cols_size, COL_CHUNKS, cols_send, cols_recv)
    finish_sends(row, rows_buf, rows_size, ROW_CHUNKS, rows_send, rows_recv)

    @pl.when(end_row)
    def _():
        finish_sends(col, crit, crit_size, CRIT_CHUNKS, crit_send, crit_recv)

    def corner_finish(chunk):
        ref = corner_ref(chunk)

        @pl.when(top_row & (col.mine == 1))
        def _():
            @pl.when(jnp.logical_not(col.last))
            def _():
                remote(
                    ref, ref, corner_csend.at[0, chunk], corner_crecv.at[chunk], col, col.next
                ).wait_send()

            remote(
                ref, ref, corner_csend.at[1, chunk], corner_crecv.at[chunk], col, col.partner
            ).wait_send()

        @pl.when(row.mine == 0)
        def _():
            @pl.when(jnp.logical_not(row.last))
            def _():
                remote(
                    ref, ref, corner_rsend.at[0, chunk], corner_rrecv.at[chunk], row, row.next
                ).wait_send()

            remote(
                ref, ref, corner_rsend.at[1, chunk], corner_rrecv.at[chunk], row, row.partner
            ).wait_send()

    loop(0, CORNER_CHUNKS, corner_finish)
    leaf_start = jnp.where((col.place == 0) & (row.mine == 1), 0, 2)
    loop(leaf_start, SLOTS, lambda s: leaf_copy(1 - row.mine, s).wait_send())

    @pl.when(jnp.logical_not(row.first))
    def _():
        loop(
            slot_start, SLOTS,
            lambda s: remote(
                part.at[row.mine, s], from_next.at[s], chain_send.at[s], next_recv.at[s],
                row, row.prev,
            ).wait_send(),
        )

    @pl.when(top_row)
    def _():
        edge_copy().wait_send()

    for copy in outs:
        copy.wait()


def update_kernel(adjoint, offdiag, rows, fix, phi, out):
    step = pl.program_id(0)
    middle = pl.num_programs(0) // 2
    width, side = phi.shape[0], fix.shape[1]
    top_row = lax.axis_index("row") == 0
    bottom_row = lax.axis_index("row") == lax.axis_size("row") - 1
    first_col = lax.axis_index("col") == 0
    last_col = lax.axis_index("col") == lax.axis_size("col") - 1
    out[...] = adjoint[...]

    @pl.when(step >= middle)
    def _():
        pairs = [split(offdiag[panel]) for panel in range(2)]
        dot = functools.partial(jnp.dot, preferred_element_type=F32)

        for start in range(0, side, width):
            value = adjoint[:, start : start + width]
            for panel, (left_high, left_low) in enumerate(pairs):
                high, low = split(rows[panel, :, start : start + width])
                value -= dot(left_high, high) + (dot(left_high, low) + dot(left_low, high))
            out[:, start : start + width] = value

        @pl.when(top_row & (step == middle))
        def _():
            out[:, :side] = out[:, :side] - fix[...]

        @pl.when(last_col)
        def _():
            out[:, side - width : side] = offdiag[1]

        @pl.when(first_col)
        def _():
            out[:, side : side + width] = offdiag[0]

            @pl.when(top_row & (step == middle))
            def _():
                out[:, side : side + width] = phi[...]

    @pl.when(bottom_row & (step == middle - 1))
    def _():
        out[:, :side] = adjoint[:, :side] - fix[...]

        @pl.when(last_col)
        def _():
            out[:, side - width : side] = phi[...]


def per_device(factor, adjoint, inverse):
    width = inverse.shape[-1]
    height, total = factor.shape
    top, side = height // 2, total // 2
    half = width // 2
    any_spec = pl.BlockSpec(memory_space=pl.ANY)
    vmem_spec = pl.BlockSpec(memory_space=pltpu.VMEM)
    dma = pltpu.SemaphoreType.DMA
    offdiag, rows, fix, phi = pl.pallas_call(
        row_kernel,
        out_shape=[
            jax.ShapeDtypeStruct((2, top, width), F32),
            jax.ShapeDtypeStruct((2, width, side), F32),
            jax.ShapeDtypeStruct((width, side), F32),
            jax.ShapeDtypeStruct((width, width), F32),
        ],
        in_specs=[any_spec, any_spec, vmem_spec],
        out_specs=[any_spec, any_spec, vmem_spec, vmem_spec],
        scratch_shapes=[
            pltpu.VMEM((top, side + width), F32),
            pltpu.VMEM((2, top, width), F32),
            pltpu.VMEM((2, top, width), F32),
            pltpu.VMEM((2, width, side), F32),
            pltpu.VMEM((width, width), F32),
            pltpu.VMEM((2, SLOTS, half, width), F32),
            pltpu.VMEM((SLOTS, half, width), F32),
            pltpu.VMEM((SLOTS, half, width), F32),
            pltpu.VMEM((2, width, width), F32),
            pltpu.VMEM((width, width), F32),
            pltpu.VMEM((width, width), F32),
            pltpu.VMEM((width, width), F32),
            pltpu.VMEM((width, width), F32),
            dma((4,)),
            dma,
            dma((2, COL_CHUNKS)),
            dma((2, COL_CHUNKS)),
            dma((CORNER_CHUNKS,)),
            dma((2, CORNER_CHUNKS)),
            dma((CORNER_CHUNKS,)),
            dma((2, CORNER_CHUNKS)),
            dma((2, ROW_CHUNKS)),
            dma((2, ROW_CHUNKS)),
            dma((SLOTS,)),
            dma((SLOTS,)),
            dma((SLOTS,)),
            dma((SLOTS,)),
            dma((2, CRIT_CHUNKS)),
            dma((2, CRIT_CHUNKS)),
            dma((2,)),
            dma((2,)),
        ],
        compiler_params=pltpu.CompilerParams(
            collective_id=0, has_side_effects=True, vmem_limit_bytes=60 * 2**20
        ),
        name="panels",
    )(factor, adjoint, inverse)
    steps = height // width
    middle = steps // 2
    return pl.pallas_call(
        update_kernel,
        grid=(steps,),
        out_shape=jax.ShapeDtypeStruct(adjoint.shape, F32),
        in_specs=[
            pl.BlockSpec((width, total), lambda t: (t, 0)),
            pl.BlockSpec((2, width, width), lambda t: (0, jnp.maximum(t - middle, 0), 0)),
            pl.BlockSpec((2, width, side), lambda t: (0, 0, 0)),
            pl.BlockSpec((width, side), lambda t: (0, 0)),
            pl.BlockSpec((width, width), lambda t: (0, 0)),
        ],
        out_specs=pl.BlockSpec((width, total), lambda t: (t, 0)),
        compiler_params=pltpu.CompilerParams(vmem_limit_bytes=60 * 2**20),
        name="update",
    )(adjoint, offdiag, rows, fix, phi)


def solution(mesh):
    return jax.shard_map(
        per_device,
        mesh=mesh,
        in_specs=(P("row", "col"), P("row", "col"), P()),
        out_specs=P("row", "col"),
        check_vma=False,
    )
```

```python
import functools

import jax
import jax.numpy as jnp
from jax import lax
from jax.experimental import pallas as pl
from jax.experimental.pallas import tpu as pltpu
from jax.sharding import PartitionSpec as P

F32 = jnp.float32
MESH = pl.DeviceIdType.MESH
SLOTS = 10
COL_CHUNKS = 4
CORNER_CHUNKS = 4
ROW_CHUNKS = 8
EARLY_CHUNKS = 4
CRIT_CHUNKS = 2


def split(value):
    high = value.astype(jnp.bfloat16)
    return high, (value - high.astype(F32)).astype(jnp.bfloat16)


def product(left, right):
    left_high, left_low = split(left)
    right_high, right_low = split(right)
    dot = functools.partial(jnp.dot, preferred_element_type=F32)
    return dot(left_high, right_high) + (dot(left_high, right_low) + dot(left_low, right_high))


def exact(left, right):
    return jnp.dot(left, right, precision=lax.Precision.HIGHEST, preferred_element_type=F32)


def iotas(width):
    rows = lax.broadcasted_iota(jnp.int32, (width, width), 0)
    cols = lax.broadcasted_iota(jnp.int32, (width, width), 1)
    return rows, cols


def halved_lower(matrix):
    rows, cols = iotas(matrix.shape[0])
    return jnp.where(rows > cols, matrix, jnp.where(rows == cols, 0.5 * matrix, 0.0))


def lower_inverse(tile):
    width = tile.shape[0]
    rows, cols = iotas(width)
    diagonal = jnp.where(rows == cols, tile, 0.0)
    power = jnp.where(rows > cols, tile, 0.0) / jnp.sum(diagonal, axis=1, keepdims=True)
    total = jnp.where(rows == cols, 1.0, 0.0) - power
    reach = 2
    while reach < width:
        power = exact(power, power)
        total = total + exact(total, power)
        reach *= 2
    return total / jnp.sum(diagonal, axis=0, keepdims=True)


def symmetric(inverse_tile, factor_diag, diag_total):
    rows, cols = iotas(inverse_tile.shape[0])
    inner = halved_lower(exact(factor_diag.T, jnp.where(rows >= cols, diag_total, 0.0)))
    wmat = exact(exact(inverse_tile.T, inner), inverse_tile)
    return wmat + wmat.T


class Line:
    def __init__(self, axis):
        self.axis = axis
        self.count = lax.axis_size(axis)
        self.place = lax.axis_index(axis)
        self.mine = lax.rem(self.place, 2)
        step = 2 - 4 * self.mine
        self.partner = self.place + 1 - 2 * self.mine
        self.prev = self.place - step
        self.next = self.place + step
        self.first = self.place == self.mine * (self.count - 1)
        self.last = self.place == (self.count - 2) * (1 - self.mine) + self.mine


def row_kernel(
    factor, adjoint, inverse, a_out, r_out, fix_out, phi_out,
    lower, cols, offdiag, rows_buf, corner, part, from_partner, from_next, crit, ldiag,
    edge_in, edge_own, dmat, local_sem, load_sem,
    cols_recv, cols_send, corner_crecv, corner_csend, corner_rrecv, corner_rsend,
    rows_recv, rows_send, leaf_send, chain_send, partner_recv, next_recv,
    crit_recv, crit_send, edge_sems, out_sem,
):
    width = inverse.shape[-1]
    half = width // 2
    top, side = cols.shape[1], rows_buf.shape[2]
    row, col = Line("row"), Line("col")
    top_row, bottom_row = row.place == 0, row.place == row.count - 1
    end_row = top_row | bottom_row

    def remote(src, dst, send, recv, line, target):
        return pltpu.make_async_remote_copy(
            src_ref=src, dst_ref=dst, send_sem=send, recv_sem=recv,
            device_id={line.axis: target}, device_id_type=MESH,
        )

    barrier = pltpu.get_barrier_semaphore()
    for line in (row, col):
        pl.semaphore_signal(barrier, inc=1, device_id={line.axis: line.partner}, device_id_type=MESH)

        @pl.when(jnp.logical_not(line.first))
        def _():
            pl.semaphore_signal(barrier, inc=1, device_id={line.axis: line.prev}, device_id_type=MESH)

        @pl.when(jnp.logical_not(line.last))
        def _():
            pl.semaphore_signal(barrier, inc=1, device_id={line.axis: line.next}, device_id_type=MESH)

    @pl.when(end_row)
    def _():
        pl.semaphore_signal(
            barrier, inc=1, device_id={"row": row.count - 1 - row.place}, device_id_type=MESH
        )

    lower_load = pltpu.make_async_copy(
        factor.at[pl.ds(top, top), pl.ds(0, side + width)], lower, load_sem
    )
    lower_load.start()
    panel_start = side - width * col.mine
    row_start = top - width * row.mine

    @pl.when(col.first)
    def _():
        copy = pltpu.make_async_copy(
            adjoint.at[pl.ds(top, top), pl.ds(pl.multiple_of(panel_start, width), width)],
            cols.at[col.mine], local_sem.at[0],
        )
        copy.start()
        copy.wait()

    @pl.when(top_row & (col.place == col.count - 1))
    def _():
        copy = pltpu.make_async_copy(
            factor.at[pl.ds(top, width), pl.ds(side - width, width)], corner, local_sem.at[1]
        )
        copy.start()
        copy.wait()

    @pl.when(row.first)
    def _():
        copy = pltpu.make_async_copy(
            factor.at[pl.ds(pl.multiple_of(row_start, width), width), pl.ds(0, side)],
            rows_buf.at[row.mine], local_sem.at[2],
        )
        copy.start()
        copy.wait()

    @pl.when(bottom_row)
    def _():
        copy = pltpu.make_async_copy(
            adjoint.at[pl.ds(top - width, width), pl.ds(side - width, width)], ldiag, local_sem.at[3]
        )
        copy.start()
        copy.wait()

    expected = 2 + sum(
        jnp.where(line.first, 0, 1) + jnp.where(line.last, 0, 1) for line in (row, col)
    )
    pl.semaphore_wait(barrier, expected + jnp.where(end_row, 1, 0))

    def pass_on(line, buf, size, chunk, recv, send, panel=None):
        lead = line.mine if panel is None else panel
        ref = buf.at[lead, pl.ds(pl.multiple_of(chunk * size, 8), size)]

        @pl.when(jnp.logical_not(line.first))
        def _():
            remote(ref, ref, send.at[0, chunk], recv.at[lead, chunk], line, line.partner).wait_recv()

        @pl.when(jnp.logical_not(line.last))
        def _():
            remote(ref, ref, send.at[0, chunk], recv.at[lead, chunk], line, line.next).start()

        remote(ref, ref, send.at[1, chunk], recv.at[lead, chunk], line, line.partner).start()

    def take(line, buf, size, chunk, recv, send):
        lead = 1 - line.mine
        ref = buf.at[lead, pl.ds(pl.multiple_of(chunk * size, 8), size)]
        remote(ref, ref, send.at[1, chunk], recv.at[lead, chunk], line, line.partner).wait_recv()

    def finish_sends(line, buf, size, chunks, send, recv):
        def body(chunk, carry):
            ref = buf.at[line.mine, pl.ds(pl.multiple_of(chunk * size, 8), size)]

            @pl.when(jnp.logical_not(line.last))
            def _():
                remote(ref, ref, send.at[0, chunk], recv.at[0, chunk], line, line.next).wait_send()

            remote(ref, ref, send.at[1, chunk], recv.at[0, chunk], line, line.partner).wait_send()
            return carry

        lax.fori_loop(0, chunks, body, 0)

    def loop(start, stop, step):
        def body(index, carry):
            step(index)
            return carry

        lax.fori_loop(start, stop, body, 0)

    cols_size = top // COL_CHUNKS
    rows_size = width // ROW_CHUNKS
    corner_size = width // CORNER_CHUNKS
    loop(0, COL_CHUNKS, lambda c: pass_on(col, cols, cols_size, c, cols_recv, cols_send))

    def corner_ref(chunk):
        return corner.at[pl.ds(pl.multiple_of(chunk * corner_size, 8), corner_size)]

    def corner_cols(chunk):
        ref = corner_ref(chunk)

        @pl.when(col.mine == 1)
        def _():
            @pl.when(jnp.logical_not(col.first))
            def _():
                remote(
                    ref, ref, corner_csend.at[0, chunk], corner_crecv.at[chunk], col, col.partner
                ).wait_recv()

            @pl.when(jnp.logical_not(col.last))
            def _():
                remote(
                    ref, ref, corner_csend.at[0, chunk], corner_crecv.at[chunk], col, col.next
                ).start()

            remote(
                ref, ref, corner_csend.at[1, chunk], corner_crecv.at[chunk], col, col.partner
            ).start()

        @pl.when(col.mine == 0)
        def _():
            remote(
                ref, ref, corner_csend.at[1, chunk], corner_crecv.at[chunk], col, col.partner
            ).wait_recv()

    def corner_rows(chunk):
        ref = corner_ref(chunk)

        @pl.when(jnp.logical_not(top_row))
        def _():
            remote(
                ref, ref, corner_rsend.at[0, chunk], corner_rrecv.at[chunk], row, row.partner
            ).wait_recv()

        @pl.when(row.mine == 0)
        def _():
            @pl.when(jnp.logical_not(row.last))
            def _():
                remote(
                    ref, ref, corner_rsend.at[0, chunk], corner_rrecv.at[chunk], row, row.next
                ).start()

            remote(
                ref, ref, corner_rsend.at[1, chunk], corner_rrecv.at[chunk], row, row.partner
            ).start()

    def corner_step(chunk):
        @pl.when(top_row)
        def _():
            corner_cols(chunk)

        corner_rows(chunk)

    def send_rows(start, stop):
        @pl.when(row.first)
        def _():
            loop(start, stop, lambda c: pass_on(row, rows_buf, rows_size, c, rows_recv, rows_send))

    send_rows(0, EARLY_CHUNKS)

    @pl.when(top_row)
    def _():
        loop(0, CORNER_CHUNKS, corner_step)

    send_rows(EARLY_CHUNKS, ROW_CHUNKS)

    loop(0, COL_CHUNKS, lambda c: take(col, cols, cols_size, c, cols_recv, cols_send))
    lower_load.wait()

    def leaf_copy(panel, slot):
        return remote(
            part.at[panel, slot], from_partner.at[slot], leaf_send.at[slot], partner_recv.at[slot],
            row, row.partner,
        )

    def own_terms(panel, first_tile, between):
        left_high, left_low = split(offdiag[panel].T)
        dot = functools.partial(jnp.dot, preferred_element_type=F32)

        def body(tile, carry):
            start = jnp.where(tile == 0, side, jnp.where(tile == 1, side - width, (tile - 2) * width))
            right = lower[:, pl.ds(pl.multiple_of(start, width), width)]
            high, low = split(right)
            value = dot(left_high, high) + (dot(left_high, low) + dot(left_low, high))
            part[panel, 2 * tile] = value[:half]
            part[panel, 2 * tile + 1] = value[half:]
            wanted = row.mine == 1 - panel
            if panel == 0:
                wanted = wanted & ((tile > 0) | (col.place == 0))

            @pl.when(wanted)
            def _():
                leaf_copy(panel, 2 * tile).start()
                leaf_copy(panel, 2 * tile + 1).start()

            between(tile)
            return carry

        lax.fori_loop(first_tile, SLOTS // 2, body, 0)

    def pass_rows(chunk):
        @pl.when((chunk < ROW_CHUNKS) & jnp.logical_not(row.first))
        def _():
            pass_on(row, rows_buf, rows_size, chunk, rows_recv, rows_send)

    def between_one(tile):
        @pl.when(tile < EARLY_CHUNKS)
        def _():
            pass_rows(tile)

        @pl.when((tile == SLOTS // 2 - 1) & jnp.logical_not(top_row))
        def _():
            loop(0, CORNER_CHUNKS, corner_step)

    slot_start = jnp.where((col.place == 0) & (row.mine == 0), 0, 2)

    def reduce_step(slot):
        mine = part.at[row.mine, slot]
        remote(
            mine, from_partner.at[slot], leaf_send.at[slot], partner_recv.at[slot], row, row.partner
        ).wait_recv()
        part[row.mine, slot] = part[row.mine, slot] + from_partner[slot]

        @pl.when(jnp.logical_not(row.last))
        def _():
            remote(
                mine, from_next.at[slot], chain_send.at[slot], next_recv.at[slot], row, row.partner
            ).wait_recv()
            part[row.mine, slot] = part[row.mine, slot] + from_next[slot]

        @pl.when(jnp.logical_not(row.first))
        def _():
            remote(
                mine, from_next.at[slot], chain_send.at[slot], next_recv.at[slot], row, row.prev
            ).start()

    offdiag[0] = product(cols[0], inverse[0])

    @pl.when(top_row)
    def _():
        offdiag[0, :width] = jnp.zeros((width, width), F32)

    own_terms(0, 0, between_one)

    early_sums = (row.mine == 0) & jnp.logical_not(row.first)

    @pl.when(early_sums)
    def _():
        loop(slot_start, 4, reduce_step)

    offdiag[1] = product(cols[1] - product(offdiag[0], corner[...]), inverse[1])

    @pl.when(top_row)
    def _():
        offdiag[1, :width] = jnp.zeros((width, width), F32)

    own_terms(1, 1, lambda tile: pass_rows(EARLY_CHUNKS - 1 + tile))
    loop(EARLY_CHUNKS + SLOTS // 2 - 1, ROW_CHUNKS, pass_rows)

    @pl.when(end_row)
    def _():
        dmat[...] = lower_inverse(inverse[row.mine])

    loop(jnp.where(early_sums, 4, slot_start), 4, reduce_step)
    crit_size = width // CRIT_CHUNKS

    @pl.when(end_row)
    def _():
        @pl.when(col.first)
        def _():
            lead = col.mine
            slot = 2 * jnp.maximum(lead, row.mine)
            for piece in range(2):
                span = slice(half * piece, half * (piece + 1))
                value = part[row.mine, slot + piece]
                crit[lead, span] = jnp.where(bottom_row, ldiag[span] - value, value)

        loop(0, CRIT_CHUNKS, lambda c: pass_on(col, crit, crit_size, c, crit_recv, crit_send))
        loop(0, CRIT_CHUNKS, lambda c: take(col, crit, crit_size, c, crit_recv, crit_send))

    def edge_copy():
        return remote(
            edge_own, edge_in, edge_sems.at[0], edge_sems.at[1], row, row.count - 1
        )

    @pl.when(top_row)
    def _():
        sym = symmetric(inverse[0], dmat[...], cols[0, :width] - crit[0])
        edge_own[...] = product(cols[1, :width] - crit[1] - product(sym, corner[...]), inverse[1])
        edge_copy().start()
        offdiag[1, :width] = edge_own[...]
        dmat[...] = sym

    loop(4, SLOTS, reduce_step)
    loop(0, ROW_CHUNKS, lambda c: take(row, rows_buf, rows_size, c, rows_recv, rows_send))

    outs = [
        pltpu.make_async_copy(offdiag, a_out, out_sem.at[0]),
        pltpu.make_async_copy(rows_buf, r_out, out_sem.at[1]),
    ]
    for copy in outs:
        copy.start()

    @pl.when(bottom_row)
    def _():
        edge_copy().wait_recv()
        edge_t = edge_in[...].T
        edge_own[...] = edge_t
        diag_total = crit[1] - product(edge_t, corner[...])
        dmat[...] = symmetric(inverse[1], dmat[...], diag_total)

    @pl.when(end_row)
    def _():
        phi_out[...] = halved_lower(dmat[...])

        def body(tile, carry):
            slot = jnp.where(tile == side // width - 1, 2, 2 * tile + 4)
            start = pl.multiple_of(tile * width, width)
            value = product(dmat[...], rows_buf[row.mine, :, pl.ds(start, width)])
            fix_out[:half, pl.ds(start, width)] = value[:half] + part[row.mine, slot]
            fix_out[half:, pl.ds(start, width)] = value[half:] + part[row.mine, slot + 1]

            @pl.when(bottom_row)
            def _():
                fix_out[:, pl.ds(start, width)] = fix_out[:, pl.ds(start, width)] + product(
                    edge_own[...], rows_buf[0, :, pl.ds(start, width)]
                )

            return carry

        lax.fori_loop(0, side // width, body, 0)

    finish_sends(col, cols, cols_size, COL_CHUNKS, cols_send, cols_recv)
    finish_sends(row, rows_buf, rows_size, ROW_CHUNKS, rows_send, rows_recv)

    @pl.when(end_row)
    def _():
        finish_sends(col, crit, crit_size, CRIT_CHUNKS, crit_send, crit_recv)

    def corner_finish(chunk):
        ref = corner_ref(chunk)

        @pl.when(top_row & (col.mine == 1))
        def _():
            @pl.when(jnp.logical_not(col.last))
            def _():
                remote(
                    ref, ref, corner_csend.at[0, chunk], corner_crecv.at[chunk], col, col.next
                ).wait_send()

            remote(
                ref, ref, corner_csend.at[1, chunk], corner_crecv.at[chunk], col, col.partner
            ).wait_send()

        @pl.when(row.mine == 0)
        def _():
            @pl.when(jnp.logical_not(row.last))
            def _():
                remote(
                    ref, ref, corner_rsend.at[0, chunk], corner_rrecv.at[chunk], row, row.next
                ).wait_send()

            remote(
                ref, ref, corner_rsend.at[1, chunk], corner_rrecv.at[chunk], row, row.partner
            ).wait_send()

    loop(0, CORNER_CHUNKS, corner_finish)
    leaf_start = jnp.where((col.place == 0) & (row.mine == 1), 0, 2)
    loop(leaf_start, SLOTS, lambda s: leaf_copy(1 - row.mine, s).wait_send())

    @pl.when(jnp.logical_not(row.first))
    def _():
        loop(
            slot_start, SLOTS,
            lambda s: remote(
                part.at[row.mine, s], from_next.at[s], chain_send.at[s], next_recv.at[s],
                row, row.prev,
            ).wait_send(),
        )

    @pl.when(top_row)
    def _():
        edge_copy().wait_send()

    for copy in outs:
        copy.wait()


def update_kernel(adjoint, offdiag, rows, fix, phi, out):
    step = pl.program_id(0)
    middle = pl.num_programs(0) // 2
    width, side = phi.shape[0], fix.shape[1]
    top_row = lax.axis_index("row") == 0
    bottom_row = lax.axis_index("row") == lax.axis_size("row") - 1
    first_col = lax.axis_index("col") == 0
    last_col = lax.axis_index("col") == lax.axis_size("col") - 1
    out[...] = adjoint[...]

    @pl.when(step >= middle)
    def _():
        pairs = [split(offdiag[panel]) for panel in range(2)]
        dot = functools.partial(jnp.dot, preferred_element_type=F32)

        for start in range(0, side, width):
            value = adjoint[:, start : start + width]
            for panel, (left_high, left_low) in enumerate(pairs):
                high, low = split(rows[panel, :, start : start + width])
                value -= dot(left_high, high) + (dot(left_high, low) + dot(left_low, high))
            out[:, start : start + width] = value

        @pl.when(top_row & (step == middle))
        def _():
            out[:, :side] = out[:, :side] - fix[...]

        @pl.when(last_col)
        def _():
            out[:, side - width : side] = offdiag[1]

        @pl.when(first_col)
        def _():
            out[:, side : side + width] = offdiag[0]

            @pl.when(top_row & (step == middle))
            def _():
                out[:, side : side + width] = phi[...]

    @pl.when(bottom_row & (step == middle - 1))
    def _():
        out[:, :side] = adjoint[:, :side] - fix[...]

        @pl.when(last_col)
        def _():
            out[:, side - width : side] = phi[...]


def per_device(factor, adjoint, inverse):
    width = inverse.shape[-1]
    height, total = factor.shape
    top, side = height // 2, total // 2
    half = width // 2
    any_spec = pl.BlockSpec(memory_space=pl.ANY)
    vmem_spec = pl.BlockSpec(memory_space=pltpu.VMEM)
    dma = pltpu.SemaphoreType.DMA
    offdiag, rows, fix, phi = pl.pallas_call(
        row_kernel,
        out_shape=[
            jax.ShapeDtypeStruct((2, top, width), F32),
            jax.ShapeDtypeStruct((2, width, side), F32),
            jax.ShapeDtypeStruct((width, side), F32),
            jax.ShapeDtypeStruct((width, width), F32),
        ],
        in_specs=[any_spec, any_spec, vmem_spec],
        out_specs=[any_spec, any_spec, vmem_spec, vmem_spec],
        scratch_shapes=[
            pltpu.VMEM((top, side + width), F32),
            pltpu.VMEM((2, top, width), F32),
            pltpu.VMEM((2, top, width), F32),
            pltpu.VMEM((2, width, side), F32),
            pltpu.VMEM((width, width), F32),
            pltpu.VMEM((2, SLOTS, half, width), F32),
            pltpu.VMEM((SLOTS, half, width), F32),
            pltpu.VMEM((SLOTS, half, width), F32),
            pltpu.VMEM((2, width, width), F32),
            pltpu.VMEM((width, width), F32),
            pltpu.VMEM((width, width), F32),
            pltpu.VMEM((width, width), F32),
            pltpu.VMEM((width, width), F32),
            dma((4,)),
            dma,
            dma((2, COL_CHUNKS)),
            dma((2, COL_CHUNKS)),
            dma((CORNER_CHUNKS,)),
            dma((2, CORNER_CHUNKS)),
            dma((CORNER_CHUNKS,)),
            dma((2, CORNER_CHUNKS)),
            dma((2, ROW_CHUNKS)),
            dma((2, ROW_CHUNKS)),
            dma((SLOTS,)),
            dma((SLOTS,)),
            dma((SLOTS,)),
            dma((SLOTS,)),
            dma((2, CRIT_CHUNKS)),
            dma((2, CRIT_CHUNKS)),
            dma((2,)),
            dma((2,)),
        ],
        compiler_params=pltpu.CompilerParams(
            collective_id=0, has_side_effects=True, vmem_limit_bytes=60 * 2**20
        ),
        name="panels",
    )(factor, adjoint, inverse)
    steps = height // width
    middle = steps // 2
    return pl.pallas_call(
        update_kernel,
        grid=(steps,),
        out_shape=jax.ShapeDtypeStruct(adjoint.shape, F32),
        in_specs=[
            pl.BlockSpec((width, total), lambda t: (t, 0)),
            pl.BlockSpec((2, width, width), lambda t: (0, jnp.maximum(t - middle, 0), 0)),
            pl.BlockSpec((2, width, side), lambda t: (0, 0, 0)),
            pl.BlockSpec((width, side), lambda t: (0, 0)),
            pl.BlockSpec((width, width), lambda t: (0, 0)),
        ],
        out_specs=pl.BlockSpec((width, total), lambda t: (t, 0)),
        compiler_params=pltpu.CompilerParams(vmem_limit_bytes=60 * 2**20),
        name="update",
    )(adjoint, offdiag, rows, fix, phi)


def solution(mesh):
    return jax.shard_map(
        per_device,
        mesh=mesh,
        in_specs=(P("row", "col"), P("row", "col"), P()),
        out_specs=P("row", "col"),
        check_vma=False,
    )
```

```python
import functools

import jax
import jax.numpy as jnp
from jax import lax
from jax.experimental import pallas as pl
from jax.experimental.pallas import tpu as pltpu
from jax.sharding import PartitionSpec as P

F32 = jnp.float32
MESH = pl.DeviceIdType.MESH
SLOTS = 10
COL_CHUNKS = 4
CORNER_CHUNKS = 4
ROW_CHUNKS = 8
EARLY_CHUNKS = 4
CRIT_CHUNKS = 2


def split(value):
    high = value.astype(jnp.bfloat16)
    return high, (value - high.astype(F32)).astype(jnp.bfloat16)


def product(left, right):
    left_high, left_low = split(left)
    right_high, right_low = split(right)
    dot = functools.partial(jnp.dot, preferred_element_type=F32)
    return dot(left_high, right_high) + (dot(left_high, right_low) + dot(left_low, right_high))


def exact(left, right):
    return jnp.dot(left, right, precision=lax.Precision.HIGHEST, preferred_element_type=F32)


def iotas(width):
    rows = lax.broadcasted_iota(jnp.int32, (width, width), 0)
    cols = lax.broadcasted_iota(jnp.int32, (width, width), 1)
    return rows, cols


def halved_lower(matrix):
    rows, cols = iotas(matrix.shape[0])
    return jnp.where(rows > cols, matrix, jnp.where(rows == cols, 0.5 * matrix, 0.0))


def lower_inverse(tile):
    width = tile.shape[0]
    rows, cols = iotas(width)
    diagonal = jnp.where(rows == cols, tile, 0.0)
    power = jnp.where(rows > cols, tile, 0.0) / jnp.sum(diagonal, axis=1, keepdims=True)
    total = jnp.where(rows == cols, 1.0, 0.0) - power
    reach = 2
    while reach < width:
        power = exact(power, power)
        total = total + exact(total, power)
        reach *= 2
    return total / jnp.sum(diagonal, axis=0, keepdims=True)


def symmetric(inverse_tile, factor_diag, diag_total):
    rows, cols = iotas(inverse_tile.shape[0])
    inner = halved_lower(exact(factor_diag.T, jnp.where(rows >= cols, diag_total, 0.0)))
    wmat = exact(exact(inverse_tile.T, inner), inverse_tile)
    return wmat + wmat.T


class Line:
    def __init__(self, axis):
        self.axis = axis
        self.count = lax.axis_size(axis)
        self.place = lax.axis_index(axis)
        self.mine = lax.rem(self.place, 2)
        step = 2 - 4 * self.mine
        self.partner = self.place + 1 - 2 * self.mine
        self.prev = self.place - step
        self.next = self.place + step
        self.first = self.place == self.mine * (self.count - 1)
        self.last = self.place == (self.count - 2) * (1 - self.mine) + self.mine


def row_kernel(
    factor, adjoint, inverse, a_out, r_out, fix_out, phi_out,
    lower, cols, offdiag, rows_buf, corner, part, from_partner, from_next, crit, ldiag,
    edge_in, edge_own, dmat, local_sem, load_sem,
    cols_recv, cols_send, corner_crecv, corner_csend, corner_rrecv, corner_rsend,
    rows_recv, rows_send, back_send, leaf_send, chain_send, partner_recv, next_recv,
    crit_recv, crit_send, edge_sems, out_sem,
):
    width = inverse.shape[-1]
    half = width // 2
    top, side = cols.shape[1], rows_buf.shape[2]
    row, col = Line("row"), Line("col")
    top_row, bottom_row = row.place == 0, row.place == row.count - 1
    end_row = top_row | bottom_row

    def remote(src, dst, send, recv, line, target):
        return pltpu.make_async_remote_copy(
            src_ref=src, dst_ref=dst, send_sem=send, recv_sem=recv,
            device_id={line.axis: target}, device_id_type=MESH,
        )

    barrier = pltpu.get_barrier_semaphore()
    for line in (row, col):
        pl.semaphore_signal(barrier, inc=1, device_id={line.axis: line.partner}, device_id_type=MESH)

        @pl.when(jnp.logical_not(line.first))
        def _():
            pl.semaphore_signal(barrier, inc=1, device_id={line.axis: line.prev}, device_id_type=MESH)

        @pl.when(jnp.logical_not(line.last))
        def _():
            pl.semaphore_signal(barrier, inc=1, device_id={line.axis: line.next}, device_id_type=MESH)

    @pl.when(end_row)
    def _():
        pl.semaphore_signal(
            barrier, inc=1, device_id={"row": row.count - 1 - row.place}, device_id_type=MESH
        )

    lower_load = pltpu.make_async_copy(
        factor.at[pl.ds(top, top), pl.ds(0, side + width)], lower, load_sem
    )
    lower_load.start()
    panel_start = side - width * col.mine
    row_start = top - width * row.mine

    @pl.when(col.first)
    def _():
        copy = pltpu.make_async_copy(
            adjoint.at[pl.ds(top, top), pl.ds(pl.multiple_of(panel_start, width), width)],
            cols.at[col.mine], local_sem.at[0],
        )
        copy.start()
        copy.wait()

    @pl.when(top_row & (col.place == col.count - 1))
    def _():
        copy = pltpu.make_async_copy(
            factor.at[pl.ds(top, width), pl.ds(side - width, width)], corner, local_sem.at[1]
        )
        copy.start()
        copy.wait()

    @pl.when(row.first)
    def _():
        copy = pltpu.make_async_copy(
            factor.at[pl.ds(pl.multiple_of(row_start, width), width), pl.ds(0, side)],
            rows_buf.at[row.mine], local_sem.at[2],
        )
        copy.start()
        copy.wait()

    @pl.when(bottom_row)
    def _():
        copy = pltpu.make_async_copy(
            adjoint.at[pl.ds(top - width, width), pl.ds(side - width, width)], ldiag, local_sem.at[3]
        )
        copy.start()
        copy.wait()

    expected = 2 + sum(
        jnp.where(line.first, 0, 1) + jnp.where(line.last, 0, 1) for line in (row, col)
    )
    pl.semaphore_wait(barrier, expected + jnp.where(end_row, 1, 0))

    def pass_on(line, buf, size, chunk, recv, send, panel=None):
        lead = line.mine if panel is None else panel
        ref = buf.at[lead, pl.ds(pl.multiple_of(chunk * size, 8), size)]

        @pl.when(jnp.logical_not(line.first))
        def _():
            remote(ref, ref, send.at[0, chunk], recv.at[lead, chunk], line, line.partner).wait_recv()

        @pl.when(jnp.logical_not(line.last))
        def _():
            remote(ref, ref, send.at[0, chunk], recv.at[lead, chunk], line, line.next).start()

        remote(ref, ref, send.at[1, chunk], recv.at[lead, chunk], line, line.partner).start()

    def take(line, buf, size, chunk, recv, send):
        lead = 1 - line.mine
        ref = buf.at[lead, pl.ds(pl.multiple_of(chunk * size, 8), size)]
        remote(ref, ref, send.at[1, chunk], recv.at[lead, chunk], line, line.partner).wait_recv()

    def finish_sends(line, buf, size, chunks, send, recv):
        def body(chunk, carry):
            ref = buf.at[line.mine, pl.ds(pl.multiple_of(chunk * size, 8), size)]

            @pl.when(jnp.logical_not(line.last))
            def _():
                remote(ref, ref, send.at[0, chunk], recv.at[0, chunk], line, line.next).wait_send()

            remote(ref, ref, send.at[1, chunk], recv.at[0, chunk], line, line.partner).wait_send()
            return carry

        lax.fori_loop(0, chunks, body, 0)

    def loop(start, stop, step):
        def body(index, carry):
            step(index)
            return carry

        lax.fori_loop(start, stop, body, 0)

    cols_size = top // COL_CHUNKS
    rows_size = width // ROW_CHUNKS
    corner_size = width // CORNER_CHUNKS
    loop(0, COL_CHUNKS, lambda c: pass_on(col, cols, cols_size, c, cols_recv, cols_send))

    def corner_ref(chunk):
        return corner.at[pl.ds(pl.multiple_of(chunk * corner_size, 8), corner_size)]

    def corner_cols(chunk):
        ref = corner_ref(chunk)

        @pl.when(col.mine == 1)
        def _():
            @pl.when(jnp.logical_not(col.first))
            def _():
                remote(
                    ref, ref, corner_csend.at[0, chunk], corner_crecv.at[chunk], col, col.partner
                ).wait_recv()

            @pl.when(jnp.logical_not(col.last))
            def _():
                remote(
                    ref, ref, corner_csend.at[0, chunk], corner_crecv.at[chunk], col, col.next
                ).start()

            remote(
                ref, ref, corner_csend.at[1, chunk], corner_crecv.at[chunk], col, col.partner
            ).start()

        @pl.when(col.mine == 0)
        def _():
            remote(
                ref, ref, corner_csend.at[1, chunk], corner_crecv.at[chunk], col, col.partner
            ).wait_recv()

    def corner_rows(chunk):
        ref = corner_ref(chunk)

        @pl.when(jnp.logical_not(top_row))
        def _():
            remote(
                ref, ref, corner_rsend.at[0, chunk], corner_rrecv.at[chunk], row, row.partner
            ).wait_recv()

        @pl.when(row.mine == 0)
        def _():
            @pl.when(jnp.logical_not(row.last))
            def _():
                remote(
                    ref, ref, corner_rsend.at[0, chunk], corner_rrecv.at[chunk], row, row.next
                ).start()

            remote(
                ref, ref, corner_rsend.at[1, chunk], corner_rrecv.at[chunk], row, row.partner
            ).start()

    def corner_step(chunk):
        @pl.when(top_row)
        def _():
            corner_cols(chunk)

        corner_rows(chunk)

    def rows_ref(panel, chunk):
        return rows_buf.at[panel, pl.ds(pl.multiple_of(chunk * rows_size, 8), rows_size)]

    def rows_copy(panel, chunk, send, target):
        ref = rows_ref(panel, chunk)
        return remote(ref, ref, send, rows_recv.at[panel, chunk], row, target)

    def rows_next(chunk):
        return rows_copy(row.mine, chunk, rows_send.at[0, chunk], row.next)

    def rows_partner(chunk):
        return rows_copy(row.mine, chunk, rows_send.at[1, chunk], row.partner)

    def rows_back(chunk):
        return rows_copy(1 - row.mine, chunk, back_send.at[chunk], row.prev)

    def pass_rows(chunk):
        @pl.when(jnp.logical_not(row.first))
        def _():
            rows_next(chunk).wait_recv()

        @pl.when(jnp.logical_not(row.last))
        def _():
            rows_next(chunk).start()

        @pl.when(row.first | (chunk < EARLY_CHUNKS))
        def _():
            rows_partner(chunk).start()

    def pass_back(chunk):
        rows_back(chunk).wait_recv()
        rows_back(chunk).start()

    def send_rows(start, stop):
        @pl.when(row.first)
        def _():
            loop(start, stop, pass_rows)

    send_rows(0, EARLY_CHUNKS)

    @pl.when(top_row)
    def _():
        loop(0, CORNER_CHUNKS, corner_step)

    send_rows(EARLY_CHUNKS, ROW_CHUNKS)

    loop(0, COL_CHUNKS, lambda c: take(col, cols, cols_size, c, cols_recv, cols_send))
    lower_load.wait()

    def leaf_copy(panel, slot):
        return remote(
            part.at[panel, slot], from_partner.at[slot], leaf_send.at[slot], partner_recv.at[slot],
            row, row.partner,
        )

    def own_terms(panel, first_tile, between):
        left_high, left_low = split(offdiag[panel].T)
        dot = functools.partial(jnp.dot, preferred_element_type=F32)

        def body(tile, carry):
            start = jnp.where(tile == 0, side, jnp.where(tile == 1, side - width, (tile - 2) * width))
            right = lower[:, pl.ds(pl.multiple_of(start, width), width)]
            high, low = split(right)
            value = dot(left_high, high) + (dot(left_high, low) + dot(left_low, high))
            part[panel, 2 * tile] = value[:half]
            part[panel, 2 * tile + 1] = value[half:]
            wanted = row.mine == 1 - panel
            if panel == 0:
                wanted = wanted & ((tile > 0) | (col.place == 0))

            @pl.when(wanted)
            def _():
                leaf_copy(panel, 2 * tile).start()
                leaf_copy(panel, 2 * tile + 1).start()

            between(tile)
            return carry

        lax.fori_loop(first_tile, SLOTS // 2, body, 0)

    def between_one(tile):
        @pl.when((tile < SLOTS // 2 - 1) & jnp.logical_not(row.first))
        def _():
            pass_rows(2 * tile)
            pass_rows(2 * tile + 1)

        @pl.when((tile == SLOTS // 2 - 1) & jnp.logical_not(top_row))
        def _():
            loop(0, CORNER_CHUNKS, corner_step)

    slot_start = jnp.where((col.place == 0) & (row.mine == 0), 0, 2)

    def reduce_step(slot):
        mine = part.at[row.mine, slot]
        remote(
            mine, from_partner.at[slot], leaf_send.at[slot], partner_recv.at[slot], row, row.partner
        ).wait_recv()
        part[row.mine, slot] = part[row.mine, slot] + from_partner[slot]

        @pl.when(jnp.logical_not(row.last))
        def _():
            remote(
                mine, from_next.at[slot], chain_send.at[slot], next_recv.at[slot], row, row.partner
            ).wait_recv()
            part[row.mine, slot] = part[row.mine, slot] + from_next[slot]

        @pl.when(jnp.logical_not(row.first))
        def _():
            remote(
                mine, from_next.at[slot], chain_send.at[slot], next_recv.at[slot], row, row.prev
            ).start()

    offdiag[0] = product(cols[0], inverse[0])

    @pl.when(top_row)
    def _():
        offdiag[0, :width] = jnp.zeros((width, width), F32)

    own_terms(0, 0, between_one)

    early_sums = (row.mine == 0) & jnp.logical_not(row.first)

    @pl.when(early_sums)
    def _():
        loop(slot_start, 4, reduce_step)

    offdiag[1] = product(cols[1] - product(offdiag[0], corner[...]), inverse[1])

    @pl.when(top_row)
    def _():
        offdiag[1, :width] = jnp.zeros((width, width), F32)

    own_terms(1, 1, lambda tile: None)

    @pl.when(jnp.logical_not(row.first))
    def _():
        loop(EARLY_CHUNKS, ROW_CHUNKS, pass_back)

    @pl.when(end_row)
    def _():
        dmat[...] = lower_inverse(inverse[row.mine])

    loop(jnp.where(early_sums, 4, slot_start), 4, reduce_step)
    crit_size = width // CRIT_CHUNKS

    @pl.when(end_row)
    def _():
        @pl.when(col.first)
        def _():
            lead = col.mine
            slot = 2 * jnp.maximum(lead, row.mine)
            for piece in range(2):
                span = slice(half * piece, half * (piece + 1))
                value = part[row.mine, slot + piece]
                crit[lead, span] = jnp.where(bottom_row, ldiag[span] - value, value)

        loop(0, CRIT_CHUNKS, lambda c: pass_on(col, crit, crit_size, c, crit_recv, crit_send))
        loop(0, CRIT_CHUNKS, lambda c: take(col, crit, crit_size, c, crit_recv, crit_send))

    def edge_copy():
        return remote(
            edge_own, edge_in, edge_sems.at[0], edge_sems.at[1], row, row.count - 1
        )

    @pl.when(top_row)
    def _():
        sym = symmetric(inverse[0], dmat[...], cols[0, :width] - crit[0])
        edge_own[...] = product(cols[1, :width] - crit[1] - product(sym, corner[...]), inverse[1])
        edge_copy().start()
        offdiag[1, :width] = edge_own[...]
        dmat[...] = sym

    loop(4, SLOTS, reduce_step)
    loop(
        0, jnp.where(row.first, ROW_CHUNKS, EARLY_CHUNKS),
        lambda c: rows_copy(1 - row.mine, c, rows_send.at[1, c], row.partner).wait_recv(),
    )

    outs = [
        pltpu.make_async_copy(offdiag, a_out, out_sem.at[0]),
        pltpu.make_async_copy(rows_buf, r_out, out_sem.at[1]),
    ]
    for copy in outs:
        copy.start()

    @pl.when(bottom_row)
    def _():
        edge_copy().wait_recv()
        edge_t = edge_in[...].T
        edge_own[...] = edge_t
        diag_total = crit[1] - product(edge_t, corner[...])
        dmat[...] = symmetric(inverse[1], dmat[...], diag_total)

    @pl.when(end_row)
    def _():
        phi_out[...] = halved_lower(dmat[...])

        def body(tile, carry):
            slot = jnp.where(tile == side // width - 1, 2, 2 * tile + 4)
            start = pl.multiple_of(tile * width, width)
            value = product(dmat[...], rows_buf[row.mine, :, pl.ds(start, width)])
            fix_out[:half, pl.ds(start, width)] = value[:half] + part[row.mine, slot]
            fix_out[half:, pl.ds(start, width)] = value[half:] + part[row.mine, slot + 1]

            @pl.when(bottom_row)
            def _():
                fix_out[:, pl.ds(start, width)] = fix_out[:, pl.ds(start, width)] + product(
                    edge_own[...], rows_buf[0, :, pl.ds(start, width)]
                )

            return carry

        lax.fori_loop(0, side // width, body, 0)

    finish_sends(col, cols, cols_size, COL_CHUNKS, cols_send, cols_recv)

    def rows_finish(chunk):
        @pl.when(jnp.logical_not(row.last))
        def _():
            rows_next(chunk).wait_send()

        @pl.when(row.first | (chunk < EARLY_CHUNKS))
        def _():
            rows_partner(chunk).wait_send()

        @pl.when(jnp.logical_not(row.first) & (chunk >= EARLY_CHUNKS))
        def _():
            rows_back(chunk).wait_send()

    loop(0, ROW_CHUNKS, rows_finish)

    @pl.when(end_row)
    def _():
        finish_sends(col, crit, crit_size, CRIT_CHUNKS, crit_send, crit_recv)

    def corner_finish(chunk):
        ref = corner_ref(chunk)

        @pl.when(top_row & (col.mine == 1))
        def _():
            @pl.when(jnp.logical_not(col.last))
            def _():
                remote(
                    ref, ref, corner_csend.at[0, chunk], corner_crecv.at[chunk], col, col.next
                ).wait_send()

            remote(
                ref, ref, corner_csend.at[1, chunk], corner_crecv.at[chunk], col, col.partner
            ).wait_send()

        @pl.when(row.mine == 0)
        def _():
            @pl.when(jnp.logical_not(row.last))
            def _():
                remote(
                    ref, ref, corner_rsend.at[0, chunk], corner_rrecv.at[chunk], row, row.next
                ).wait_send()

            remote(
                ref, ref, corner_rsend.at[1, chunk], corner_rrecv.at[chunk], row, row.partner
            ).wait_send()

    loop(0, CORNER_CHUNKS, corner_finish)
    leaf_start = jnp.where((col.place == 0) & (row.mine == 1), 0, 2)
    loop(leaf_start, SLOTS, lambda s: leaf_copy(1 - row.mine, s).wait_send())

    @pl.when(jnp.logical_not(row.first))
    def _():
        loop(
            slot_start, SLOTS,
            lambda s: remote(
                part.at[row.mine, s], from_next.at[s], chain_send.at[s], next_recv.at[s],
                row, row.prev,
            ).wait_send(),
        )

    @pl.when(top_row)
    def _():
        edge_copy().wait_send()

    for copy in outs:
        copy.wait()


def update_kernel(adjoint, offdiag, rows, fix, phi, out, high, low):
    step = pl.program_id(0)
    middle = pl.num_programs(0) // 2
    width, side = phi.shape[0], fix.shape[1]
    top_row = lax.axis_index("row") == 0
    bottom_row = lax.axis_index("row") == lax.axis_size("row") - 1
    first_col = lax.axis_index("col") == 0
    last_col = lax.axis_index("col") == lax.axis_size("col") - 1
    out[...] = adjoint[...]

    for panel in range(2):

        @pl.when(step == panel)
        def _():
            span = slice(panel * width, (panel + 1) * width)
            high[span], low[span] = split(rows[panel])

    @pl.when(step >= middle)
    def _():
        left_high, left_low = split(jnp.concatenate([offdiag[0], offdiag[1]], axis=1))
        dot = functools.partial(jnp.dot, preferred_element_type=F32)

        for start in range(0, side, width):
            span = slice(start, start + width)
            out[:, span] = adjoint[:, span] - (
                dot(left_high, high[:, span])
                + (dot(left_high, low[:, span]) + dot(left_low, high[:, span]))
            )

        @pl.when(top_row & (step == middle))
        def _():
            out[:, :side] = out[:, :side] - fix[...]

        @pl.when(last_col)
        def _():
            out[:, side - width : side] = offdiag[1]

        @pl.when(first_col)
        def _():
            out[:, side : side + width] = offdiag[0]

            @pl.when(top_row & (step == middle))
            def _():
                out[:, side : side + width] = phi[...]

    @pl.when(bottom_row & (step == middle - 1))
    def _():
        out[:, :side] = adjoint[:, :side] - fix[...]

        @pl.when(last_col)
        def _():
            out[:, side - width : side] = phi[...]


def per_device(factor, adjoint, inverse):
    width = inverse.shape[-1]
    height, total = factor.shape
    top, side = height // 2, total // 2
    half = width // 2
    any_spec = pl.BlockSpec(memory_space=pl.ANY)
    vmem_spec = pl.BlockSpec(memory_space=pltpu.VMEM)
    dma = pltpu.SemaphoreType.DMA
    offdiag, rows, fix, phi = pl.pallas_call(
        row_kernel,
        out_shape=[
            jax.ShapeDtypeStruct((2, top, width), F32),
            jax.ShapeDtypeStruct((2, width, side), F32),
            jax.ShapeDtypeStruct((width, side), F32),
            jax.ShapeDtypeStruct((width, width), F32),
        ],
        in_specs=[any_spec, any_spec, vmem_spec],
        out_specs=[any_spec, any_spec, vmem_spec, vmem_spec],
        scratch_shapes=[
            pltpu.VMEM((top, side + width), F32),
            pltpu.VMEM((2, top, width), F32),
            pltpu.VMEM((2, top, width), F32),
            pltpu.VMEM((2, width, side), F32),
            pltpu.VMEM((width, width), F32),
            pltpu.VMEM((2, SLOTS, half, width), F32),
            pltpu.VMEM((SLOTS, half, width), F32),
            pltpu.VMEM((SLOTS, half, width), F32),
            pltpu.VMEM((2, width, width), F32),
            pltpu.VMEM((width, width), F32),
            pltpu.VMEM((width, width), F32),
            pltpu.VMEM((width, width), F32),
            pltpu.VMEM((width, width), F32),
            dma((4,)),
            dma,
            dma((2, COL_CHUNKS)),
            dma((2, COL_CHUNKS)),
            dma((CORNER_CHUNKS,)),
            dma((2, CORNER_CHUNKS)),
            dma((CORNER_CHUNKS,)),
            dma((2, CORNER_CHUNKS)),
            dma((2, ROW_CHUNKS)),
            dma((2, ROW_CHUNKS)),
            dma((ROW_CHUNKS,)),
            dma((SLOTS,)),
            dma((SLOTS,)),
            dma((SLOTS,)),
            dma((SLOTS,)),
            dma((2, CRIT_CHUNKS)),
            dma((2, CRIT_CHUNKS)),
            dma((2,)),
            dma((2,)),
        ],
        compiler_params=pltpu.CompilerParams(
            collective_id=0, has_side_effects=True, vmem_limit_bytes=60 * 2**20
        ),
        name="panels",
    )(factor, adjoint, inverse)
    steps = height // width
    middle = steps // 2
    return pl.pallas_call(
        update_kernel,
        grid=(steps,),
        out_shape=jax.ShapeDtypeStruct(adjoint.shape, F32),
        in_specs=[
            pl.BlockSpec((width, total), lambda t: (t, 0)),
            pl.BlockSpec((2, width, width), lambda t: (0, jnp.maximum(t - middle, 0), 0)),
            pl.BlockSpec((2, width, side), lambda t: (0, 0, 0)),
            pl.BlockSpec((width, side), lambda t: (0, 0)),
            pl.BlockSpec((width, width), lambda t: (0, 0)),
        ],
        out_specs=pl.BlockSpec((width, total), lambda t: (t, 0)),
        scratch_shapes=[pltpu.VMEM((2 * width, side), jnp.bfloat16)] * 2,
        compiler_params=pltpu.CompilerParams(vmem_limit_bytes=60 * 2**20),
        name="update",
    )(adjoint, offdiag, rows, fix, phi)


def solution(mesh):
    return jax.shard_map(
        per_device,
        mesh=mesh,
        in_specs=(P("row", "col"), P("row", "col"), P()),
        out_specs=P("row", "col"),
        check_vma=False,
    )
```

```python
import functools

import jax
import jax.numpy as jnp
from jax import lax
from jax.experimental import pallas as pl
from jax.experimental.pallas import tpu as pltpu
from jax.sharding import PartitionSpec as P

F32 = jnp.float32
MESH = pl.DeviceIdType.MESH
SLOTS = 10
COL_CHUNKS = 4
CORNER_CHUNKS = 4
ROW_CHUNKS = 8
EARLY_CHUNKS = 2
CRIT_CHUNKS = 2


def split(value):
    high = value.astype(jnp.bfloat16)
    return high, (value - high.astype(F32)).astype(jnp.bfloat16)


def product(left, right):
    left_high, left_low = split(left)
    right_high, right_low = split(right)
    dot = functools.partial(jnp.dot, preferred_element_type=F32)
    return dot(left_high, right_high) + (dot(left_high, right_low) + dot(left_low, right_high))


def exact(left, right):
    return jnp.dot(left, right, precision=lax.Precision.HIGHEST, preferred_element_type=F32)


def iotas(width):
    rows = lax.broadcasted_iota(jnp.int32, (width, width), 0)
    cols = lax.broadcasted_iota(jnp.int32, (width, width), 1)
    return rows, cols


def halved_lower(matrix):
    rows, cols = iotas(matrix.shape[0])
    return jnp.where(rows > cols, matrix, jnp.where(rows == cols, 0.5 * matrix, 0.0))


def lower_inverse(tile):
    width = tile.shape[0]
    rows, cols = iotas(width)
    diagonal = jnp.where(rows == cols, tile, 0.0)
    power = jnp.where(rows > cols, tile, 0.0) / jnp.sum(diagonal, axis=1, keepdims=True)
    total = jnp.where(rows == cols, 1.0, 0.0) - power
    reach = 2
    while reach < width:
        power = exact(power, power)
        total = total + exact(total, power)
        reach *= 2
    return total / jnp.sum(diagonal, axis=0, keepdims=True)


def symmetric(inverse_tile, factor_diag, diag_total):
    rows, cols = iotas(inverse_tile.shape[0])
    inner = halved_lower(exact(factor_diag.T, jnp.where(rows >= cols, diag_total, 0.0)))
    wmat = exact(exact(inverse_tile.T, inner), inverse_tile)
    return wmat + wmat.T


class Line:
    def __init__(self, axis):
        self.axis = axis
        self.count = lax.axis_size(axis)
        self.place = lax.axis_index(axis)
        self.mine = lax.rem(self.place, 2)
        step = 2 - 4 * self.mine
        self.partner = self.place + 1 - 2 * self.mine
        self.prev = self.place - step
        self.next = self.place + step
        self.first = self.place == self.mine * (self.count - 1)
        self.last = self.place == (self.count - 2) * (1 - self.mine) + self.mine


def row_kernel(
    factor, adjoint, inverse, a_out, r_out, fix_out, phi_out,
    lower, cols, offdiag, rows_buf, corner, part, from_partner, from_next, crit, ldiag,
    edge_in, edge_own, dmat, local_sem, load_sem,
    cols_recv, cols_send, corner_crecv, corner_csend, corner_rrecv, corner_rsend,
    rows_recv, rows_send, leaf_send, chain_send, partner_recv, next_recv,
    crit_recv, crit_send, edge_sems, out_sem,
):
    width = inverse.shape[-1]
    half = width // 2
    top, side = cols.shape[1], rows_buf.shape[2]
    row, col = Line("row"), Line("col")
    top_row, bottom_row = row.place == 0, row.place == row.count - 1
    end_row = top_row | bottom_row

    def remote(src, dst, send, recv, line, target):
        return pltpu.make_async_remote_copy(
            src_ref=src, dst_ref=dst, send_sem=send, recv_sem=recv,
            device_id={line.axis: target}, device_id_type=MESH,
        )

    barrier = pltpu.get_barrier_semaphore()
    for line in (row, col):
        pl.semaphore_signal(barrier, inc=1, device_id={line.axis: line.partner}, device_id_type=MESH)

        @pl.when(jnp.logical_not(line.first))
        def _():
            pl.semaphore_signal(barrier, inc=1, device_id={line.axis: line.prev}, device_id_type=MESH)

        @pl.when(jnp.logical_not(line.last))
        def _():
            pl.semaphore_signal(barrier, inc=1, device_id={line.axis: line.next}, device_id_type=MESH)

    @pl.when(end_row)
    def _():
        pl.semaphore_signal(
            barrier, inc=1, device_id={"row": row.count - 1 - row.place}, device_id_type=MESH
        )

    lower_load = pltpu.make_async_copy(
        factor.at[pl.ds(top, top), pl.ds(0, side + width)], lower, load_sem
    )
    lower_load.start()
    panel_start = side - width * col.mine
    row_start = top - width * row.mine

    @pl.when(col.first)
    def _():
        copy = pltpu.make_async_copy(
            adjoint.at[pl.ds(top, top), pl.ds(pl.multiple_of(panel_start, width), width)],
            cols.at[col.mine], local_sem.at[0],
        )
        copy.start()
        copy.wait()

    @pl.when(top_row & (col.place == col.count - 1))
    def _():
        copy = pltpu.make_async_copy(
            factor.at[pl.ds(top, width), pl.ds(side - width, width)], corner, local_sem.at[1]
        )
        copy.start()
        copy.wait()

    @pl.when(row.first)
    def _():
        copy = pltpu.make_async_copy(
            factor.at[pl.ds(pl.multiple_of(row_start, width), width), pl.ds(0, side)],
            rows_buf.at[row.mine], local_sem.at[2],
        )
        copy.start()
        copy.wait()

    @pl.when(bottom_row)
    def _():
        copy = pltpu.make_async_copy(
            adjoint.at[pl.ds(top - width, width), pl.ds(side - width, width)], ldiag, local_sem.at[3]
        )
        copy.start()
        copy.wait()

    expected = 2 + sum(
        jnp.where(line.first, 0, 1) + jnp.where(line.last, 0, 1) for line in (row, col)
    )
    pl.semaphore_wait(barrier, expected + jnp.where(end_row, 1, 0))

    def pass_on(line, buf, size, chunk, recv, send, panel=None):
        lead = line.mine if panel is None else panel
        ref = buf.at[lead, pl.ds(pl.multiple_of(chunk * size, 8), size)]

        @pl.when(jnp.logical_not(line.first))
        def _():
            remote(ref, ref, send.at[0, chunk], recv.at[lead, chunk], line, line.partner).wait_recv()

        @pl.when(jnp.logical_not(line.last))
        def _():
            remote(ref, ref, send.at[0, chunk], recv.at[lead, chunk], line, line.next).start()

        remote(ref, ref, send.at[1, chunk], recv.at[lead, chunk], line, line.partner).start()

    def take(line, buf, size, chunk, recv, send):
        lead = 1 - line.mine
        ref = buf.at[lead, pl.ds(pl.multiple_of(chunk * size, 8), size)]
        remote(ref, ref, send.at[1, chunk], recv.at[lead, chunk], line, line.partner).wait_recv()

    def finish_sends(line, buf, size, chunks, send, recv):
        def body(chunk, carry):
            ref = buf.at[line.mine, pl.ds(pl.multiple_of(chunk * size, 8), size)]

            @pl.when(jnp.logical_not(line.last))
            def _():
                remote(ref, ref, send.at[0, chunk], recv.at[0, chunk], line, line.next).wait_send()

            remote(ref, ref, send.at[1, chunk], recv.at[0, chunk], line, line.partner).wait_send()
            return carry

        lax.fori_loop(0, chunks, body, 0)

    def loop(start, stop, step):
        def body(index, carry):
            step(index)
            return carry

        lax.fori_loop(start, stop, body, 0)

    cols_size = top // COL_CHUNKS
    rows_size = width // ROW_CHUNKS
    corner_size = width // CORNER_CHUNKS

    def corner_ref(chunk):
        return corner.at[pl.ds(pl.multiple_of(chunk * corner_size, 8), corner_size)]

    def corner_cols(chunk):
        ref = corner_ref(chunk)

        @pl.when(col.mine == 1)
        def _():
            @pl.when(jnp.logical_not(col.first))
            def _():
                remote(
                    ref, ref, corner_csend.at[0, chunk], corner_crecv.at[chunk], col, col.partner
                ).wait_recv()

            @pl.when(jnp.logical_not(col.last))
            def _():
                remote(
                    ref, ref, corner_csend.at[0, chunk], corner_crecv.at[chunk], col, col.next
                ).start()

            remote(
                ref, ref, corner_csend.at[1, chunk], corner_crecv.at[chunk], col, col.partner
            ).start()

        @pl.when(col.mine == 0)
        def _():
            remote(
                ref, ref, corner_csend.at[1, chunk], corner_crecv.at[chunk], col, col.partner
            ).wait_recv()

    @pl.when(top_row & (col.place == col.count - 1))
    def _():
        loop(0, CORNER_CHUNKS, corner_cols)

    loop(0, COL_CHUNKS, lambda c: pass_on(col, cols, cols_size, c, cols_recv, cols_send))

    def corner_rows(chunk):
        ref = corner_ref(chunk)

        @pl.when(jnp.logical_not(top_row))
        def _():
            remote(
                ref, ref, corner_rsend.at[0, chunk], corner_rrecv.at[chunk], row, row.partner
            ).wait_recv()

        @pl.when(row.mine == 0)
        def _():
            @pl.when(jnp.logical_not(row.last))
            def _():
                remote(
                    ref, ref, corner_rsend.at[0, chunk], corner_rrecv.at[chunk], row, row.next
                ).start()

            remote(
                ref, ref, corner_rsend.at[1, chunk], corner_rrecv.at[chunk], row, row.partner
            ).start()

    def corner_step(chunk):
        @pl.when(top_row & jnp.logical_not(col.place == col.count - 1))
        def _():
            corner_cols(chunk)

        corner_rows(chunk)

    def send_rows(start, stop):
        @pl.when(row.first)
        def _():
            loop(start, stop, lambda c: pass_on(row, rows_buf, rows_size, c, rows_recv, rows_send))

    send_rows(0, EARLY_CHUNKS)

    @pl.when(top_row)
    def _():
        loop(0, CORNER_CHUNKS, corner_step)

    send_rows(EARLY_CHUNKS, ROW_CHUNKS)

    loop(0, COL_CHUNKS, lambda c: take(col, cols, cols_size, c, cols_recv, cols_send))
    lower_load.wait()

    def leaf_copy(panel, slot):
        return remote(
            part.at[panel, slot], from_partner.at[slot], leaf_send.at[slot], partner_recv.at[slot],
            row, row.partner,
        )

    def own_terms(panel, first_tile, between):
        left_high, left_low = split(offdiag[panel].T)
        dot = functools.partial(jnp.dot, preferred_element_type=F32)

        def body(tile, carry):
            start = jnp.where(tile == 0, side, jnp.where(tile == 1, side - width, (tile - 2) * width))
            right = lower[:, pl.ds(pl.multiple_of(start, width), width)]
            high, low = split(right)
            value = dot(left_high, high) + (dot(left_high, low) + dot(left_low, high))
            part[panel, 2 * tile] = value[:half]
            part[panel, 2 * tile + 1] = value[half:]
            wanted = row.mine == 1 - panel
            if panel == 0:
                wanted = wanted & ((tile > 0) | (col.place == 0))

            @pl.when(wanted)
            def _():
                leaf_copy(panel, 2 * tile).start()
                leaf_copy(panel, 2 * tile + 1).start()

            between(tile)
            return carry

        lax.fori_loop(first_tile, SLOTS // 2, body, 0)

    def pass_rows(chunk):
        @pl.when((chunk < ROW_CHUNKS) & jnp.logical_not(row.first))
        def _():
            pass_on(row, rows_buf, rows_size, chunk, rows_recv, rows_send)

    def between_one(tile):
        @pl.when((tile == EARLY_CHUNKS) & jnp.logical_not(top_row))
        def _():
            loop(0, CORNER_CHUNKS, corner_step)

        pass_rows(tile)

    slot_start = jnp.where((col.place == 0) & (row.mine == 0), 0, 2)

    def reduce_step(slot):
        mine = part.at[row.mine, slot]
        remote(
            mine, from_partner.at[slot], leaf_send.at[slot], partner_recv.at[slot], row, row.partner
        ).wait_recv()
        part[row.mine, slot] = part[row.mine, slot] + from_partner[slot]

        @pl.when(jnp.logical_not(row.last))
        def _():
            remote(
                mine, from_next.at[slot], chain_send.at[slot], next_recv.at[slot], row, row.partner
            ).wait_recv()
            part[row.mine, slot] = part[row.mine, slot] + from_next[slot]

        @pl.when(jnp.logical_not(row.first))
        def _():
            remote(
                mine, from_next.at[slot], chain_send.at[slot], next_recv.at[slot], row, row.prev
            ).start()

    offdiag[0] = product(cols[0], inverse[0])

    @pl.when(top_row)
    def _():
        offdiag[0, :width] = jnp.zeros((width, width), F32)

    own_terms(0, 0, between_one)

    offdiag[1] = product(cols[1] - product(offdiag[0], corner[...]), inverse[1])

    @pl.when(top_row)
    def _():
        offdiag[1, :width] = jnp.zeros((width, width), F32)

    own_terms(1, 1, lambda tile: pass_rows(SLOTS // 2 - 1 + tile))
    loop(SLOTS - 1, ROW_CHUNKS, pass_rows)

    @pl.when(end_row)
    def _():
        dmat[...] = lower_inverse(inverse[row.mine])

    loop(slot_start, 4, reduce_step)
    crit_size = width // CRIT_CHUNKS

    @pl.when(end_row)
    def _():
        @pl.when(col.first)
        def _():
            lead = col.mine
            slot = 2 * jnp.maximum(lead, row.mine)
            for piece in range(2):
                span = slice(half * piece, half * (piece + 1))
                value = part[row.mine, slot + piece]
                crit[lead, span] = jnp.where(bottom_row, ldiag[span] - value, value)

        loop(0, CRIT_CHUNKS, lambda c: pass_on(col, crit, crit_size, c, crit_recv, crit_send))
        loop(0, CRIT_CHUNKS, lambda c: take(col, crit, crit_size, c, crit_recv, crit_send))

    def edge_copy():
        return remote(
            edge_own, edge_in, edge_sems.at[0], edge_sems.at[1], row, row.count - 1
        )

    @pl.when(top_row)
    def _():
        sym = symmetric(inverse[0], dmat[...], cols[0, :width] - crit[0])
        edge_own[...] = product(cols[1, :width] - crit[1] - product(sym, corner[...]), inverse[1])
        edge_copy().start()
        offdiag[1, :width] = edge_own[...]
        dmat[...] = sym

    loop(4, SLOTS, reduce_step)
    loop(0, ROW_CHUNKS, lambda c: take(row, rows_buf, rows_size, c, rows_recv, rows_send))

    outs = [
        pltpu.make_async_copy(offdiag, a_out, out_sem.at[0]),
        pltpu.make_async_copy(rows_buf, r_out, out_sem.at[1]),
    ]
    for copy in outs:
        copy.start()

    @pl.when(bottom_row)
    def _():
        edge_copy().wait_recv()
        edge_t = edge_in[...].T
        edge_own[...] = edge_t
        diag_total = crit[1] - product(edge_t, corner[...])
        dmat[...] = symmetric(inverse[1], dmat[...], diag_total)

    @pl.when(end_row)
    def _():
        phi_out[...] = halved_lower(dmat[...])

        def body(tile, carry):
            slot = jnp.where(tile == side // width - 1, 2, 2 * tile + 4)
            start = pl.multiple_of(tile * width, width)
            value = product(dmat[...], rows_buf[row.mine, :, pl.ds(start, width)])
            fix_out[:half, pl.ds(start, width)] = value[:half] + part[row.mine, slot]
            fix_out[half:, pl.ds(start, width)] = value[half:] + part[row.mine, slot + 1]

            @pl.when(bottom_row)
            def _():
                fix_out[:, pl.ds(start, width)] = fix_out[:, pl.ds(start, width)] + product(
                    edge_own[...], rows_buf[0, :, pl.ds(start, width)]
                )

            return carry

        lax.fori_loop(0, side // width, body, 0)

    finish_sends(col, cols, cols_size, COL_CHUNKS, cols_send, cols_recv)
    finish_sends(row, rows_buf, rows_size, ROW_CHUNKS, rows_send, rows_recv)

    @pl.when(end_row)
    def _():
        finish_sends(col, crit, crit_size, CRIT_CHUNKS, crit_send, crit_recv)

    def corner_finish(chunk):
        ref = corner_ref(chunk)

        @pl.when(top_row & (col.mine == 1))
        def _():
            @pl.when(jnp.logical_not(col.last))
            def _():
                remote(
                    ref, ref, corner_csend.at[0, chunk], corner_crecv.at[chunk], col, col.next
                ).wait_send()

            remote(
                ref, ref, corner_csend.at[1, chunk], corner_crecv.at[chunk], col, col.partner
            ).wait_send()

        @pl.when(row.mine == 0)
        def _():
            @pl.when(jnp.logical_not(row.last))
            def _():
                remote(
                    ref, ref, corner_rsend.at[0, chunk], corner_rrecv.at[chunk], row, row.next
                ).wait_send()

            remote(
                ref, ref, corner_rsend.at[1, chunk], corner_rrecv.at[chunk], row, row.partner
            ).wait_send()

    loop(0, CORNER_CHUNKS, corner_finish)
    leaf_start = jnp.where((col.place == 0) & (row.mine == 1), 0, 2)
    loop(leaf_start, SLOTS, lambda s: leaf_copy(1 - row.mine, s).wait_send())

    @pl.when(jnp.logical_not(row.first))
    def _():
        loop(
            slot_start, SLOTS,
            lambda s: remote(
                part.at[row.mine, s], from_next.at[s], chain_send.at[s], next_recv.at[s],
                row, row.prev,
            ).wait_send(),
        )

    @pl.when(top_row)
    def _():
        edge_copy().wait_send()

    for copy in outs:
        copy.wait()


def update_kernel(adjoint, offdiag, rows, fix, phi, out):
    step = pl.program_id(0)
    middle = pl.num_programs(0) // 2
    width, side = phi.shape[0], fix.shape[1]
    top_row = lax.axis_index("row") == 0
    bottom_row = lax.axis_index("row") == lax.axis_size("row") - 1
    first_col = lax.axis_index("col") == 0
    last_col = lax.axis_index("col") == lax.axis_size("col") - 1
    out[...] = adjoint[...]

    @pl.when(step >= middle)
    def _():
        pairs = [split(offdiag[panel]) for panel in range(2)]
        dot = functools.partial(jnp.dot, preferred_element_type=F32)

        for start in range(0, side, width):
            value = adjoint[:, start : start + width]
            for panel, (left_high, left_low) in enumerate(pairs):
                high, low = split(rows[panel, :, start : start + width])
                value -= dot(left_high, high) + (dot(left_high, low) + dot(left_low, high))
            out[:, start : start + width] = value

        @pl.when(top_row & (step == middle))
        def _():
            out[:, :side] = out[:, :side] - fix[...]

        @pl.when(last_col)
        def _():
            out[:, side - width : side] = offdiag[1]

        @pl.when(first_col)
        def _():
            out[:, side : side + width] = offdiag[0]

            @pl.when(top_row & (step == middle))
            def _():
                out[:, side : side + width] = phi[...]

    @pl.when(bottom_row & (step == middle - 1))
    def _():
        out[:, :side] = adjoint[:, :side] - fix[...]

        @pl.when(last_col)
        def _():
            out[:, side - width : side] = phi[...]


def per_device(factor, adjoint, inverse):
    width = inverse.shape[-1]
    height, total = factor.shape
    top, side = height // 2, total // 2
    half = width // 2
    any_spec = pl.BlockSpec(memory_space=pl.ANY)
    vmem_spec = pl.BlockSpec(memory_space=pltpu.VMEM)
    dma = pltpu.SemaphoreType.DMA
    offdiag, rows, fix, phi = pl.pallas_call(
        row_kernel,
        out_shape=[
            jax.ShapeDtypeStruct((2, top, width), F32),
            jax.ShapeDtypeStruct((2, width, side), F32),
            jax.ShapeDtypeStruct((width, side), F32),
            jax.ShapeDtypeStruct((width, width), F32),
        ],
        in_specs=[any_spec, any_spec, vmem_spec],
        out_specs=[any_spec, any_spec, vmem_spec, vmem_spec],
        scratch_shapes=[
            pltpu.VMEM((top, side + width), F32),
            pltpu.VMEM((2, top, width), F32),
            pltpu.VMEM((2, top, width), F32),
            pltpu.VMEM((2, width, side), F32),
            pltpu.VMEM((width, width), F32),
            pltpu.VMEM((2, SLOTS, half, width), F32),
            pltpu.VMEM((SLOTS, half, width), F32),
            pltpu.VMEM((SLOTS, half, width), F32),
            pltpu.VMEM((2, width, width), F32),
            pltpu.VMEM((width, width), F32),
            pltpu.VMEM((width, width), F32),
            pltpu.VMEM((width, width), F32),
            pltpu.VMEM((width, width), F32),
            dma((4,)),
            dma,
            dma((2, COL_CHUNKS)),
            dma((2, COL_CHUNKS)),
            dma((CORNER_CHUNKS,)),
            dma((2, CORNER_CHUNKS)),
            dma((CORNER_CHUNKS,)),
            dma((2, CORNER_CHUNKS)),
            dma((2, ROW_CHUNKS)),
            dma((2, ROW_CHUNKS)),
            dma((SLOTS,)),
            dma((SLOTS,)),
            dma((SLOTS,)),
            dma((SLOTS,)),
            dma((2, CRIT_CHUNKS)),
            dma((2, CRIT_CHUNKS)),
            dma((2,)),
            dma((2,)),
        ],
        compiler_params=pltpu.CompilerParams(
            collective_id=0, has_side_effects=True, vmem_limit_bytes=60 * 2**20
        ),
        name="panels",
    )(factor, adjoint, inverse)
    steps = height // width
    middle = steps // 2
    return pl.pallas_call(
        update_kernel,
        grid=(steps,),
        out_shape=jax.ShapeDtypeStruct(adjoint.shape, F32),
        in_specs=[
            pl.BlockSpec((width, total), lambda t: (t, 0)),
            pl.BlockSpec((2, width, width), lambda t: (0, jnp.maximum(t - middle, 0), 0)),
            pl.BlockSpec((2, width, side), lambda t: (0, 0, 0)),
            pl.BlockSpec((width, side), lambda t: (0, 0)),
            pl.BlockSpec((width, width), lambda t: (0, 0)),
        ],
        out_specs=pl.BlockSpec((width, total), lambda t: (t, 0)),
        compiler_params=pltpu.CompilerParams(vmem_limit_bytes=60 * 2**20),
        name="update",
    )(adjoint, offdiag, rows, fix, phi)


def solution(mesh):
    return jax.shard_map(
        per_device,
        mesh=mesh,
        in_specs=(P("row", "col"), P("row", "col"), P()),
        out_specs=P("row", "col"),
        check_vma=False,
    )
```

```python
import functools

import jax
import jax.numpy as jnp
from jax import lax
from jax.experimental import pallas as pl
from jax.experimental.pallas import tpu as pltpu
from jax.sharding import PartitionSpec as P

F32 = jnp.float32
MESH = pl.DeviceIdType.MESH
SLOTS = 10
COL_CHUNKS = 4
CORNER_CHUNKS = 4
ROW_CHUNKS = 8
EARLY_CHUNKS = 2
CRIT_CHUNKS = 2


def split(value):
    high = value.astype(jnp.bfloat16)
    return high, (value - high.astype(F32)).astype(jnp.bfloat16)


def product(left, right):
    left_high, left_low = split(left)
    right_high, right_low = split(right)
    dot = functools.partial(jnp.dot, preferred_element_type=F32)
    return dot(left_high, right_high) + (dot(left_high, right_low) + dot(left_low, right_high))


def exact(left, right):
    return jnp.dot(left, right, precision=lax.Precision.HIGHEST, preferred_element_type=F32)


def iotas(width):
    rows = lax.broadcasted_iota(jnp.int32, (width, width), 0)
    cols = lax.broadcasted_iota(jnp.int32, (width, width), 1)
    return rows, cols


def halved_lower(matrix):
    rows, cols = iotas(matrix.shape[0])
    return jnp.where(rows > cols, matrix, jnp.where(rows == cols, 0.5 * matrix, 0.0))


def lower_inverse(tile):
    width = tile.shape[0]
    rows, cols = iotas(width)
    diagonal = jnp.where(rows == cols, tile, 0.0)
    power = jnp.where(rows > cols, tile, 0.0) / jnp.sum(diagonal, axis=1, keepdims=True)
    total = jnp.where(rows == cols, 1.0, 0.0) - power
    reach = 2
    while reach < width:
        power = exact(power, power)
        total = total + exact(total, power)
        reach *= 2
    return total / jnp.sum(diagonal, axis=0, keepdims=True)


def symmetric(inverse_tile, factor_diag, diag_total):
    rows, cols = iotas(inverse_tile.shape[0])
    inner = halved_lower(exact(factor_diag.T, jnp.where(rows >= cols, diag_total, 0.0)))
    wmat = exact(exact(inverse_tile.T, inner), inverse_tile)
    return wmat + wmat.T


class Line:
    def __init__(self, axis):
        self.axis = axis
        self.count = lax.axis_size(axis)
        self.place = lax.axis_index(axis)
        self.mine = lax.rem(self.place, 2)
        step = 2 - 4 * self.mine
        self.partner = self.place + 1 - 2 * self.mine
        self.prev = self.place - step
        self.next = self.place + step
        self.first = self.place == self.mine * (self.count - 1)
        self.last = self.place == (self.count - 2) * (1 - self.mine) + self.mine


def row_kernel(
    factor, adjoint, inverse, a_out, r_out, fix_out, phi_out,
    lower, cols, offdiag, rows_buf, corner, part, from_partner, from_next, crit, ldiag,
    edge_in, edge_own, dmat, local_sem, load_sem,
    cols_recv, cols_send, corner_crecv, corner_csend, corner_rrecv, corner_rsend,
    rows_recv, rows_send, leaf_send, chain_send, partner_recv, next_recv,
    crit_recv, crit_send, edge_sems, out_sem,
):
    width = inverse.shape[-1]
    half = width // 2
    top, side = cols.shape[1], rows_buf.shape[2]
    row, col = Line("row"), Line("col")
    top_row, bottom_row = row.place == 0, row.place == row.count - 1
    end_row = top_row | bottom_row

    def remote(src, dst, send, recv, line, target):
        return pltpu.make_async_remote_copy(
            src_ref=src, dst_ref=dst, send_sem=send, recv_sem=recv,
            device_id={line.axis: target}, device_id_type=MESH,
        )

    barrier = pltpu.get_barrier_semaphore()
    for line in (row, col):
        pl.semaphore_signal(barrier, inc=1, device_id={line.axis: line.partner}, device_id_type=MESH)

        @pl.when(jnp.logical_not(line.first))
        def _():
            pl.semaphore_signal(barrier, inc=1, device_id={line.axis: line.prev}, device_id_type=MESH)

        @pl.when(jnp.logical_not(line.last))
        def _():
            pl.semaphore_signal(barrier, inc=1, device_id={line.axis: line.next}, device_id_type=MESH)

    @pl.when(end_row)
    def _():
        pl.semaphore_signal(
            barrier, inc=1, device_id={"row": row.count - 1 - row.place}, device_id_type=MESH
        )

    lower_load = pltpu.make_async_copy(
        factor.at[pl.ds(top, top), pl.ds(0, side + width)], lower, load_sem
    )
    lower_load.start()
    panel_start = side - width * col.mine
    row_start = top - width * row.mine

    @pl.when(col.first)
    def _():
        copy = pltpu.make_async_copy(
            adjoint.at[pl.ds(top, top), pl.ds(pl.multiple_of(panel_start, width), width)],
            cols.at[col.mine], local_sem.at[0],
        )
        copy.start()
        copy.wait()

    @pl.when(top_row & (col.place == col.count - 1))
    def _():
        copy = pltpu.make_async_copy(
            factor.at[pl.ds(top, width), pl.ds(side - width, width)], corner, local_sem.at[1]
        )
        copy.start()
        copy.wait()

    @pl.when(row.first)
    def _():
        copy = pltpu.make_async_copy(
            factor.at[pl.ds(pl.multiple_of(row_start, width), width), pl.ds(0, side)],
            rows_buf.at[row.mine], local_sem.at[2],
        )
        copy.start()
        copy.wait()

    @pl.when(bottom_row)
    def _():
        copy = pltpu.make_async_copy(
            adjoint.at[pl.ds(top - width, width), pl.ds(side - width, width)], ldiag, local_sem.at[3]
        )
        copy.start()
        copy.wait()

    expected = 2 + sum(
        jnp.where(line.first, 0, 1) + jnp.where(line.last, 0, 1) for line in (row, col)
    )
    pl.semaphore_wait(barrier, expected + jnp.where(end_row, 1, 0))

    def pass_on(line, buf, size, chunk, recv, send, panel=None):
        lead = line.mine if panel is None else panel
        ref = buf.at[lead, pl.ds(pl.multiple_of(chunk * size, 8), size)]

        @pl.when(jnp.logical_not(line.first))
        def _():
            remote(ref, ref, send.at[0, chunk], recv.at[lead, chunk], line, line.partner).wait_recv()

        @pl.when(jnp.logical_not(line.last))
        def _():
            remote(ref, ref, send.at[0, chunk], recv.at[lead, chunk], line, line.next).start()

        remote(ref, ref, send.at[1, chunk], recv.at[lead, chunk], line, line.partner).start()

    def take(line, buf, size, chunk, recv, send):
        lead = 1 - line.mine
        ref = buf.at[lead, pl.ds(pl.multiple_of(chunk * size, 8), size)]
        remote(ref, ref, send.at[1, chunk], recv.at[lead, chunk], line, line.partner).wait_recv()

    def finish_sends(line, buf, size, chunks, send, recv):
        def body(chunk, carry):
            ref = buf.at[line.mine, pl.ds(pl.multiple_of(chunk * size, 8), size)]

            @pl.when(jnp.logical_not(line.last))
            def _():
                remote(ref, ref, send.at[0, chunk], recv.at[0, chunk], line, line.next).wait_send()

            remote(ref, ref, send.at[1, chunk], recv.at[0, chunk], line, line.partner).wait_send()
            return carry

        lax.fori_loop(0, chunks, body, 0)

    def loop(start, stop, step):
        def body(index, carry):
            step(index)
            return carry

        lax.fori_loop(start, stop, body, 0)

    cols_size = top // COL_CHUNKS
    rows_size = width // ROW_CHUNKS
    corner_size = width // CORNER_CHUNKS

    def corner_ref(chunk):
        return corner.at[pl.ds(pl.multiple_of(chunk * corner_size, 8), corner_size)]

    def corner_cols(chunk):
        ref = corner_ref(chunk)

        @pl.when(col.mine == 1)
        def _():
            @pl.when(jnp.logical_not(col.first))
            def _():
                remote(
                    ref, ref, corner_csend.at[0, chunk], corner_crecv.at[chunk], col, col.partner
                ).wait_recv()

            @pl.when(jnp.logical_not(col.last))
            def _():
                remote(
                    ref, ref, corner_csend.at[0, chunk], corner_crecv.at[chunk], col, col.next
                ).start()

            remote(
                ref, ref, corner_csend.at[1, chunk], corner_crecv.at[chunk], col, col.partner
            ).start()

        @pl.when(col.mine == 0)
        def _():
            remote(
                ref, ref, corner_csend.at[1, chunk], corner_crecv.at[chunk], col, col.partner
            ).wait_recv()

    @pl.when(top_row & (col.place == col.count - 1))
    def _():
        loop(0, CORNER_CHUNKS, corner_cols)

    def pass_cols():
        loop(0, COL_CHUNKS, lambda c: pass_on(col, cols, cols_size, c, cols_recv, cols_send))

    @pl.when(col.first)
    def _():
        pass_cols()

    def corner_rows(chunk):
        ref = corner_ref(chunk)

        @pl.when(jnp.logical_not(top_row))
        def _():
            remote(
                ref, ref, corner_rsend.at[0, chunk], corner_rrecv.at[chunk], row, row.partner
            ).wait_recv()

        @pl.when(row.mine == 0)
        def _():
            @pl.when(jnp.logical_not(row.last))
            def _():
                remote(
                    ref, ref, corner_rsend.at[0, chunk], corner_rrecv.at[chunk], row, row.next
                ).start()

            remote(
                ref, ref, corner_rsend.at[1, chunk], corner_rrecv.at[chunk], row, row.partner
            ).start()

    def corner_step(chunk):
        @pl.when(top_row & jnp.logical_not(col.place == col.count - 1))
        def _():
            corner_cols(chunk)

        corner_rows(chunk)

    def send_rows(start, stop):
        @pl.when(row.first)
        def _():
            loop(start, stop, lambda c: pass_on(row, rows_buf, rows_size, c, rows_recv, rows_send))

    send_rows(0, EARLY_CHUNKS)

    @pl.when(top_row)
    def _():
        loop(0, CORNER_CHUNKS, corner_step)

    @pl.when(jnp.logical_not(col.first))
    def _():
        pass_cols()

    send_rows(EARLY_CHUNKS, ROW_CHUNKS)

    loop(0, COL_CHUNKS, lambda c: take(col, cols, cols_size, c, cols_recv, cols_send))
    lower_load.wait()

    def leaf_copy(panel, slot):
        return remote(
            part.at[panel, slot], from_partner.at[slot], leaf_send.at[slot], partner_recv.at[slot],
            row, row.partner,
        )

    def own_terms(panel, first_tile, between):
        left_high, left_low = split(offdiag[panel].T)
        dot = functools.partial(jnp.dot, preferred_element_type=F32)

        def body(tile, carry):
            start = jnp.where(tile == 0, side, jnp.where(tile == 1, side - width, (tile - 2) * width))
            right = lower[:, pl.ds(pl.multiple_of(start, width), width)]
            high, low = split(right)
            value = dot(left_high, high) + (dot(left_high, low) + dot(left_low, high))
            part[panel, 2 * tile] = value[:half]
            part[panel, 2 * tile + 1] = value[half:]
            wanted = row.mine == 1 - panel
            if panel == 0:
                wanted = wanted & ((tile > 0) | (col.place == 0))

            @pl.when(wanted)
            def _():
                leaf_copy(panel, 2 * tile).start()
                leaf_copy(panel, 2 * tile + 1).start()

            between(tile)
            return carry

        lax.fori_loop(first_tile, SLOTS // 2, body, 0)

    def pass_rows(chunk):
        @pl.when((chunk < ROW_CHUNKS) & jnp.logical_not(row.first))
        def _():
            pass_on(row, rows_buf, rows_size, chunk, rows_recv, rows_send)

    def between_one(tile):
        @pl.when((tile == EARLY_CHUNKS) & jnp.logical_not(top_row))
        def _():
            loop(0, CORNER_CHUNKS, corner_step)

        pass_rows(tile)

    slot_start = jnp.where((col.place == 0) & (row.mine == 0), 0, 2)

    def reduce_step(slot):
        mine = part.at[row.mine, slot]
        remote(
            mine, from_partner.at[slot], leaf_send.at[slot], partner_recv.at[slot], row, row.partner
        ).wait_recv()
        part[row.mine, slot] = part[row.mine, slot] + from_partner[slot]

        @pl.when(jnp.logical_not(row.last))
        def _():
            remote(
                mine, from_next.at[slot], chain_send.at[slot], next_recv.at[slot], row, row.partner
            ).wait_recv()
            part[row.mine, slot] = part[row.mine, slot] + from_next[slot]

        @pl.when(jnp.logical_not(row.first))
        def _():
            remote(
                mine, from_next.at[slot], chain_send.at[slot], next_recv.at[slot], row, row.prev
            ).start()

    offdiag[0] = product(cols[0], inverse[0])

    @pl.when(top_row)
    def _():
        offdiag[0, :width] = jnp.zeros((width, width), F32)

    own_terms(0, 0, between_one)

    offdiag[1] = product(cols[1] - product(offdiag[0], corner[...]), inverse[1])

    @pl.when(top_row)
    def _():
        offdiag[1, :width] = jnp.zeros((width, width), F32)

    own_terms(1, 1, lambda tile: pass_rows(SLOTS // 2 - 1 + tile))
    loop(SLOTS - 1, ROW_CHUNKS, pass_rows)

    @pl.when(end_row)
    def _():
        dmat[...] = lower_inverse(inverse[row.mine])

    loop(slot_start, 4, reduce_step)
    crit_size = width // CRIT_CHUNKS

    @pl.when(end_row)
    def _():
        @pl.when(col.first)
        def _():
            lead = col.mine
            slot = 2 * jnp.maximum(lead, row.mine)
            for piece in range(2):
                span = slice(half * piece, half * (piece + 1))
                value = part[row.mine, slot + piece]
                crit[lead, span] = jnp.where(bottom_row, ldiag[span] - value, value)

        loop(0, CRIT_CHUNKS, lambda c: pass_on(col, crit, crit_size, c, crit_recv, crit_send))
        loop(0, CRIT_CHUNKS, lambda c: take(col, crit, crit_size, c, crit_recv, crit_send))

    def edge_copy():
        return remote(
            edge_own, edge_in, edge_sems.at[0], edge_sems.at[1], row, row.count - 1
        )

    @pl.when(top_row)
    def _():
        sym = symmetric(inverse[0], dmat[...], cols[0, :width] - crit[0])
        edge_own[...] = product(cols[1, :width] - crit[1] - product(sym, corner[...]), inverse[1])
        edge_copy().start()
        offdiag[1, :width] = edge_own[...]
        dmat[...] = sym

    loop(4, SLOTS, reduce_step)
    loop(0, ROW_CHUNKS, lambda c: take(row, rows_buf, rows_size, c, rows_recv, rows_send))

    outs = [
        pltpu.make_async_copy(offdiag, a_out, out_sem.at[0]),
        pltpu.make_async_copy(rows_buf, r_out, out_sem.at[1]),
    ]
    for copy in outs:
        copy.start()

    @pl.when(bottom_row)
    def _():
        edge_copy().wait_recv()
        edge_t = edge_in[...].T
        edge_own[...] = edge_t
        diag_total = crit[1] - product(edge_t, corner[...])
        dmat[...] = symmetric(inverse[1], dmat[...], diag_total)

    @pl.when(end_row)
    def _():
        phi_out[...] = halved_lower(dmat[...])

        def body(tile, carry):
            slot = jnp.where(tile == side // width - 1, 2, 2 * tile + 4)
            start = pl.multiple_of(tile * width, width)
            value = product(dmat[...], rows_buf[row.mine, :, pl.ds(start, width)])
            fix_out[:half, pl.ds(start, width)] = value[:half] + part[row.mine, slot]
            fix_out[half:, pl.ds(start, width)] = value[half:] + part[row.mine, slot + 1]

            @pl.when(bottom_row)
            def _():
                fix_out[:, pl.ds(start, width)] = fix_out[:, pl.ds(start, width)] + product(
                    edge_own[...], rows_buf[0, :, pl.ds(start, width)]
                )

            return carry

        lax.fori_loop(0, side // width, body, 0)

    finish_sends(col, cols, cols_size, COL_CHUNKS, cols_send, cols_recv)
    finish_sends(row, rows_buf, rows_size, ROW_CHUNKS, rows_send, rows_recv)

    @pl.when(end_row)
    def _():
        finish_sends(col, crit, crit_size, CRIT_CHUNKS, crit_send, crit_recv)

    def corner_finish(chunk):
        ref = corner_ref(chunk)

        @pl.when(top_row & (col.mine == 1))
        def _():
            @pl.when(jnp.logical_not(col.last))
            def _():
                remote(
                    ref, ref, corner_csend.at[0, chunk], corner_crecv.at[chunk], col, col.next
                ).wait_send()

            remote(
                ref, ref, corner_csend.at[1, chunk], corner_crecv.at[chunk], col, col.partner
            ).wait_send()

        @pl.when(row.mine == 0)
        def _():
            @pl.when(jnp.logical_not(row.last))
            def _():
                remote(
                    ref, ref, corner_rsend.at[0, chunk], corner_rrecv.at[chunk], row, row.next
                ).wait_send()

            remote(
                ref, ref, corner_rsend.at[1, chunk], corner_rrecv.at[chunk], row, row.partner
            ).wait_send()

    loop(0, CORNER_CHUNKS, corner_finish)
    leaf_start = jnp.where((col.place == 0) & (row.mine == 1), 0, 2)
    loop(leaf_start, SLOTS, lambda s: leaf_copy(1 - row.mine, s).wait_send())

    @pl.when(jnp.logical_not(row.first))
    def _():
        loop(
            slot_start, SLOTS,
            lambda s: remote(
                part.at[row.mine, s], from_next.at[s], chain_send.at[s], next_recv.at[s],
                row, row.prev,
            ).wait_send(),
        )

    @pl.when(top_row)
    def _():
        edge_copy().wait_send()

    for copy in outs:
        copy.wait()


def update_kernel(adjoint, offdiag, rows, fix, phi, out):
    step = pl.program_id(0)
    middle = pl.num_programs(0) // 2
    width, side = phi.shape[0], fix.shape[1]
    top_row = lax.axis_index("row") == 0
    bottom_row = lax.axis_index("row") == lax.axis_size("row") - 1
    first_col = lax.axis_index("col") == 0
    last_col = lax.axis_index("col") == lax.axis_size("col") - 1
    out[...] = adjoint[...]

    @pl.when(step >= middle)
    def _():
        pairs = [split(offdiag[panel]) for panel in range(2)]
        dot = functools.partial(jnp.dot, preferred_element_type=F32)

        for start in range(0, side, width):
            value = adjoint[:, start : start + width]
            for panel, (left_high, left_low) in enumerate(pairs):
                high, low = split(rows[panel, :, start : start + width])
                value -= dot(left_high, high) + (dot(left_high, low) + dot(left_low, high))
            out[:, start : start + width] = value

        @pl.when(top_row & (step == middle))
        def _():
            out[:, :side] = out[:, :side] - fix[...]

        @pl.when(last_col)
        def _():
            out[:, side - width : side] = offdiag[1]

        @pl.when(first_col)
        def _():
            out[:, side : side + width] = offdiag[0]

            @pl.when(top_row & (step == middle))
            def _():
                out[:, side : side + width] = phi[...]

    @pl.when(bottom_row & (step == middle - 1))
    def _():
        out[:, :side] = adjoint[:, :side] - fix[...]

        @pl.when(last_col)
        def _():
            out[:, side - width : side] = phi[...]


def per_device(factor, adjoint, inverse):
    width = inverse.shape[-1]
    height, total = factor.shape
    top, side = height // 2, total // 2
    half = width // 2
    any_spec = pl.BlockSpec(memory_space=pl.ANY)
    vmem_spec = pl.BlockSpec(memory_space=pltpu.VMEM)
    dma = pltpu.SemaphoreType.DMA
    offdiag, rows, fix, phi = pl.pallas_call(
        row_kernel,
        out_shape=[
            jax.ShapeDtypeStruct((2, top, width), F32),
            jax.ShapeDtypeStruct((2, width, side), F32),
            jax.ShapeDtypeStruct((width, side), F32),
            jax.ShapeDtypeStruct((width, width), F32),
        ],
        in_specs=[any_spec, any_spec, vmem_spec],
        out_specs=[any_spec, any_spec, vmem_spec, vmem_spec],
        scratch_shapes=[
            pltpu.VMEM((top, side + width), F32),
            pltpu.VMEM((2, top, width), F32),
            pltpu.VMEM((2, top, width), F32),
            pltpu.VMEM((2, width, side), F32),
            pltpu.VMEM((width, width), F32),
            pltpu.VMEM((2, SLOTS, half, width), F32),
            pltpu.VMEM((SLOTS, half, width), F32),
            pltpu.VMEM((SLOTS, half, width), F32),
            pltpu.VMEM((2, width, width), F32),
            pltpu.VMEM((width, width), F32),
            pltpu.VMEM((width, width), F32),
            pltpu.VMEM((width, width), F32),
            pltpu.VMEM((width, width), F32),
            dma((4,)),
            dma,
            dma((2, COL_CHUNKS)),
            dma((2, COL_CHUNKS)),
            dma((CORNER_CHUNKS,)),
            dma((2, CORNER_CHUNKS)),
            dma((CORNER_CHUNKS,)),
            dma((2, CORNER_CHUNKS)),
            dma((2, ROW_CHUNKS)),
            dma((2, ROW_CHUNKS)),
            dma((SLOTS,)),
            dma((SLOTS,)),
            dma((SLOTS,)),
            dma((SLOTS,)),
            dma((2, CRIT_CHUNKS)),
            dma((2, CRIT_CHUNKS)),
            dma((2,)),
            dma((2,)),
        ],
        compiler_params=pltpu.CompilerParams(
            collective_id=0, has_side_effects=True, vmem_limit_bytes=60 * 2**20
        ),
        name="panels",
    )(factor, adjoint, inverse)
    steps = height // width
    middle = steps // 2
    return pl.pallas_call(
        update_kernel,
        grid=(steps,),
        out_shape=jax.ShapeDtypeStruct(adjoint.shape, F32),
        in_specs=[
            pl.BlockSpec((width, total), lambda t: (t, 0)),
            pl.BlockSpec((2, width, width), lambda t: (0, jnp.maximum(t - middle, 0), 0)),
            pl.BlockSpec((2, width, side), lambda t: (0, 0, 0)),
            pl.BlockSpec((width, side), lambda t: (0, 0)),
            pl.BlockSpec((width, width), lambda t: (0, 0)),
        ],
        out_specs=pl.BlockSpec((width, total), lambda t: (t, 0)),
        compiler_params=pltpu.CompilerParams(vmem_limit_bytes=60 * 2**20),
        name="update",
    )(adjoint, offdiag, rows, fix, phi)


def solution(mesh):
    return jax.shard_map(
        per_device,
        mesh=mesh,
        in_specs=(P("row", "col"), P("row", "col"), P()),
        out_specs=P("row", "col"),
        check_vma=False,
    )
```
